128 devices in a mesh: trial: 32 (over z_hi, y, x), batch: 4 (over z_lo, core).
Axes of the slice: x: 4, y: 4, z: 4 (z_hi: 2, z_lo: 2; z = z_hi * 2 + z_lo), core: 2. Of those that a mesh axis runs over, the one named last changes fastest.
Arguments:
- features16: bfloat16 [32, 4, 1024, 512], P('trial', 'batch'), may hold values from -6 to 6
- features32: bfloat16 [32, 4, 2048, 128], P('trial', 'batch'), may hold values from -6 to 6
- labels: int32 [32, 4, 512], P(None, 'batch'), may hold values from 0 to 18
- plan: int32 [4], replicated, may hold values from 0 to 31, as said below
- lr_index: int32 [32], P('trial'), may hold values from 0 to 1073741823
- w_plain: float32 [32, 256, 1024], P('trial'), may hold values from -0.1875 to 0.1875
- w_depth: float32 [32, 3, 9, 1024], P('trial'), may hold values from -2 to 2
- w_point: float32 [32, 3, 256, 1024], P('trial'), may hold values from -0.1875 to 0.1875
- w_pool: float32 [32, 256, 2048], P('trial'), may hold values from -0.125 to 0.125
- b_branch: float32 [32, 5, 256], P('trial'), may hold values from -3 to 3
- w_proj: float32 [32, 256, 1280], P('trial'), may hold values from -0.15625 to 0.15625
- b_proj: float32 [32, 256], P('trial'), may hold values from -3 to 3
- w_class: float32 [32, 19, 256], P('trial'), may hold values from -1 to 4
- b_class: float32 [32, 19], P('trial'), may hold values from -4 to 4
Outputs:
- new_w_plain: float32 [32, 256, 1024], P('trial')
- new_w_depth: float32 [32, 3, 9, 1024], P('trial')
- new_w_point: float32 [32, 3, 256, 1024], P('trial')
- new_w_pool: float32 [32, 256, 2048], P('trial')
- new_b_branch: float32 [32, 5, 256], P('trial')
- new_w_proj: float32 [32, 256, 1280], P('trial')
- new_b_proj: float32 [32, 256], P('trial')
- new_w_class: float32 [32, 19, 256], P('trial')
- new_b_class: float32 [32, 19], P('trial')
The draws below stay inside these ranges and needn't reach their ends.
Inputs may be any that keep to these rules, and one draw needn't show every extreme that they name: `plan`: the 4 entries are distinct trial indices; 0 and 31 are always among them.
All inputs are finite; a program needn't handle non-finite values.
Results may differ from the reference program's by a relative error of at most 0.014.
The reference program's roundings to bfloat16 on the way count: a program that leaves them out, or rounds other values in their place, can miss the bound.
Values may be sent and summed in bfloat16 or wider, within the bound.
No kernel may reach another device: no remote copies, remote signals or barrier semaphores. Data moves between devices by JAX's collectives and lax.ppermute only.
A program may use at most 128 MiB of HBM per device.

```python
import jax
import jax.numpy as jnp
from jax import lax

C16 = 1024
C32 = 2048
HID = 256
CLASSES = 19
W16 = 32
MICRO = 4
IMG_DEV = 1
P16 = 512
P32 = 128
TRIALS = 32
IMAGES_B = 4
N_BATCH = 4


def draw_plan(key, part):
    subkeys = jax.random.split(key, 2)
    others = jax.random.permutation(subkeys[0], TRIALS - 2).astype(jnp.int32) + 1
    ends = jnp.array([0, TRIALS - 1], dtype=jnp.int32)
    picks = jnp.concatenate([ends, others[:MICRO - 2]])
    order = jax.random.permutation(subkeys[1], MICRO)
    return picks[order].astype(jnp.int32)


def draw_w_class(key, part):
    subkeys = jax.random.split(key, 1)
    spread_factor = HID ** (-0.5)
    matrix = jnp.clip(jax.random.normal(subkeys[0], (TRIALS, CLASSES, HID), jnp.float32), -6.0, 6.0) * spread_factor
    return matrix.astype(jnp.float32)


def touch_ends(drawn, rng, low, high):
    extent = drawn.shape
    place = [jax.random.randint(jax.random.fold_in(rng, axis), (), 0, extent[axis]) for axis in range(len(extent))]
    drawn = drawn.at[tuple(place)].set(low)
    longest = extent.index(max(extent))
    place[longest] = (place[longest] + 1) % extent[longest]
    return drawn.at[tuple(place)].set(high)


def block_levels(own_key, shape, pieces, low, largest):
    def one(dim, parts):
        draws = jax.random.uniform(jax.random.fold_in(jax.random.fold_in(own_key, 6), dim), (parts,), jnp.float32, low / len(pieces), largest / len(pieces))
        return jnp.repeat(jnp.exp(draws), shape[dim] // parts).reshape((-1,) + (1,) * (len(shape) - dim - 1))

    gain = one(*pieces[0])
    for cut in pieces[1:]:
        gain = gain * one(*cut)
    return gain


def gaussian(key, shape, spread, bound, shards=(), kind=jnp.bfloat16):
    drawn = spread * jax.random.normal(key, shape, jnp.float32)
    if shards:
        drawn = drawn * block_levels(key, shape, shards, -0.22, 0.18)
    return jnp.clip(drawn, -bound, bound).astype(kind)


def setup_inputs(seed: int = 0) -> dict:
    key_of = jax.random.split(jax.random.key(seed), 15)
    return {
        "features16": gaussian(key_of[0], (TRIALS, IMAGES_B, C16, P16), 1.0, 6.0, ((0, 32), (1, 4))),
        "features32": gaussian(key_of[1], (TRIALS, IMAGES_B, C32, P32), 1.0, 6.0, ((0, 32), (1, 4))),
        "labels": touch_ends(jax.random.randint(key_of[2], (TRIALS, IMAGES_B, P16), 0, CLASSES), jax.random.fold_in(key_of[2], 1), 0, CLASSES - 1).astype(jnp.int32),
        "plan": draw_plan(jax.random.fold_in(key_of[14], 71), 0),
        "lr_index": touch_ends(jax.random.randint(key_of[4], (TRIALS,), 0, 1073741824), jax.random.fold_in(key_of[4], 1), 0, 1073741823).astype(jnp.int32),
        "w_plain": gaussian(key_of[5], (TRIALS, HID, C16), C16 ** -0.5, 0.1875, ((0, 32),), jnp.float32),
        "w_depth": gaussian(key_of[6], (TRIALS, 3, 9, C16), 9 ** -0.5, 2.0, ((0, 32),), jnp.float32),
        "w_point": gaussian(key_of[7], (TRIALS, 3, HID, C16), C16 ** -0.5, 0.1875, ((0, 32),), jnp.float32),
        "w_pool": gaussian(key_of[8], (TRIALS, HID, C32), C32 ** -0.5, 0.125, ((0, 32),), jnp.float32),
        "b_branch": gaussian(key_of[9], (TRIALS, 5, HID), 0.5, 3.0, ((0, 32),), jnp.float32),
        "w_proj": gaussian(key_of[10], (TRIALS, HID, 5 * HID), (5 * HID) ** -0.5, 0.15625, ((0, 32),), jnp.float32),
        "b_proj": gaussian(key_of[11], (TRIALS, HID), 0.5, 3.0, ((0, 32),), jnp.float32),
        "w_class": draw_w_class(jax.random.fold_in(key_of[14], 71), 0),
        "b_class": gaussian(key_of[13], (TRIALS, CLASSES), 1.0, 4.0, ((0, 32),), jnp.float32),
    }


dilations = (6, 12, 18)

def shifted_tap(feature_map, vertical, across):
    pixels = feature_map.shape[1]
    offset = vertical * W16 + across
    if offset == 0:
        shifted = feature_map
    else:
        margin = abs(offset)
        padded = jnp.pad(feature_map, ((0, 0), (margin, margin)))
        shifted = lax.slice_in_dim(padded, margin + offset, margin + offset + pixels, axis=1)
    column = jnp.arange(pixels, dtype=jnp.int32) % W16 + across
    inside = ((column >= 0) & (column < W16)).astype(jnp.float32)
    return (shifted, inside)

def depthwise(feature_map, tap_weights, dilation):
    summed = jnp.zeros(feature_map.shape, jnp.float32)
    for vertical in (-1, 0, 1):
        for across in (-1, 0, 1):
            shifted, inside = shifted_tap(feature_map, vertical * dilation, across * dilation)
            weight_row = tap_weights[3 * (vertical + 1) + (across + 1)]
            summed = summed + weight_row[:, None] * shifted * inside[None, :]
    return summed

def head_loss(params, feature_map, pooled, targets):
    w_plain, w_depth, w_point, w_pool, b_branch, w_proj, b_proj, w_class, b_class = params
    branches = [jax.nn.relu(jnp.dot(w_plain.astype(jnp.bfloat16), feature_map, preferred_element_type=jnp.float32) + b_branch[0][:, None])]
    for branch_id, dilation in enumerate(dilations):
        depth_map = depthwise(feature_map, w_depth[branch_id], dilation).astype(jnp.bfloat16)
        branches.append(jax.nn.relu(jnp.dot(w_point[branch_id].astype(jnp.bfloat16), depth_map, preferred_element_type=jnp.float32) + b_branch[branch_id + 1][:, None]))
    pooled_out = jax.nn.relu(jnp.dot(w_pool.astype(jnp.bfloat16), pooled, preferred_element_type=jnp.float32) + b_branch[4])
    branches.append(jnp.broadcast_to(pooled_out[:, None], branches[0].shape))
    joined = jnp.concatenate(branches, axis=0).astype(jnp.bfloat16)
    hidden = jax.nn.relu(jnp.dot(w_proj.astype(jnp.bfloat16), joined, preferred_element_type=jnp.float32) + b_proj[:, None]).astype(jnp.bfloat16)
    logits = jnp.dot(w_class.astype(jnp.bfloat16), hidden, preferred_element_type=jnp.float32) + b_class[:, None]
    class_ids = jnp.arange(logits.shape[0], dtype=jnp.int32)
    chosen = lax.optimization_barrier(jnp.sum(jnp.where(class_ids[:, None] == targets[None, :], logits, 0.0), axis=0))
    return jnp.sum(jax.nn.logsumexp(logits, axis=0) - chosen)

def reference(features16, features32, labels, plan, lr_index, w_plain, w_depth, w_point, w_pool, b_branch, w_proj, b_proj, w_class, b_class):
    weights = (w_plain, w_depth, w_point, w_pool, b_branch, w_proj, b_proj, w_class, b_class)
    grad_image = jax.grad(head_loss)

    def one_trial(trial):
        params = tuple((lax.dynamic_index_in_dim(weight, trial, 0, keepdims=False) for weight in weights))
        summed = tuple((jnp.zeros(weight.shape, jnp.float32) for weight in params))
        for group in range(N_BATCH):
            partial_value = tuple((jnp.zeros(weight.shape, jnp.float32) for weight in params))
            for turn_index in range(MICRO):
                owner = plan[turn_index]
                maps = lax.dynamic_index_in_dim(features16, owner, 0, keepdims=False)
                coarse = lax.dynamic_index_in_dim(features32, owner, 0, keepdims=False)
                marks = lax.dynamic_index_in_dim(labels, owner, 0, keepdims=False)

                def add_image(carried, slot_index):
                    picture = group * IMG_DEV + slot_index
                    feature_map = lax.dynamic_index_in_dim(maps, picture, 0, keepdims=False)
                    coarse_map = lax.dynamic_index_in_dim(coarse, picture, 0, keepdims=False)
                    targets = lax.dynamic_index_in_dim(marks, picture, 0, keepdims=False)
                    pooled = (lax.optimization_barrier(jnp.sum(coarse_map, axis=-1, dtype=jnp.float32)) / coarse_map.shape[-1]).astype(jnp.bfloat16)
                    gradient = grad_image(params, feature_map, pooled, targets)
                    return (tuple((before + after for before, after in zip(carried, gradient))), None)
                partial_value, _ = lax.scan(add_image, partial_value, jnp.arange(IMG_DEV, dtype=jnp.int32))
            rounded = lax.optimization_barrier(tuple((value.astype(jnp.bfloat16) for value in partial_value)))
            summed = tuple((before + value.astype(jnp.float32) for before, value in zip(summed, rounded)))
        squares = sum((jnp.sum(gradient * gradient) for gradient in summed))
        entries = sum((gradient.size for gradient in summed))
        norm_scale = jnp.sqrt(squares / entries + 1e-06)
        index_value = lax.dynamic_index_in_dim(lr_index, trial, 0, keepdims=False)
        step_rate = 0.5 * jnp.exp2(-6.0 * index_value.astype(jnp.float32) / 1073741824.0)
        return tuple((weight - step_rate * gradient / norm_scale for weight, gradient in zip(params, summed)))
    updated = lax.map(one_trial, jnp.arange(TRIALS, dtype=jnp.int32))
    return (updated[0], updated[1], updated[2], updated[3], updated[4], updated[5], updated[6], updated[7], updated[8])
```

```python
import functools

import jax
import jax.numpy as jnp
from jax import lax
from jax.experimental import pallas as pl
from jax.experimental.pallas import tpu as pltpu
from jax.sharding import PartitionSpec as P

W16 = 32
HID = 256
PAD = 24
DILATIONS = (6, 12, 18)
LANES = 128
RELATIVE = (0, -1, 1, 2)
BF16 = jnp.bfloat16
F32 = jnp.float32


def dot_nt(a, b):
    return lax.dot_general(a, b, (((1,), (1,)), ((), ())), preferred_element_type=F32)


def dot_nn(a, b):
    return lax.dot_general(a, b, (((1,), (0,)), ((), ())), preferred_element_type=F32)


def dot_tn(a, b):
    return lax.dot_general(a, b, (((0,), (0,)), ((), ())), preferred_element_type=F32)


def taps_of_row(row, rows, dilation):
    taps = []
    for a in (-1, 0, 1):
        source = row + a * dilation
        if 0 <= source < rows:
            for b in (-1, 0, 1):
                taps.append((3 * (a + 1) + (b + 1), source, b * dilation))
    return taps


def clear_margins(padded):
    rows = padded.shape[0]
    blank = jnp.zeros((rows, PAD, LANES), F32)
    padded[:, 0:PAD, :] = blank
    padded[:, PAD + W16 : 2 * PAD + W16, :] = blank


def fill_padded(padded, x_ref, lanes):
    for row in range(padded.shape[0]):
        padded[row, PAD : PAD + W16, :] = x_ref[row * W16 : (row + 1) * W16, lanes].astype(F32)


def front_kernel(
    order,
    where_ref,
    piece0,
    piece1,
    piece2,
    piece3,
    marks,
    w_plain,
    w_depth,
    w_point,
    bias,
    w_proj,
    proj_bias,
    w_class,
    class_bias,
    x_ref,
    depth_ref,
    joined_ref,
    dpre_ref,
    dz_ref,
    sums_ref,
    dclass_ref,
    dclass_bias_ref,
    padded,
):
    x, y, z = where_ref[0], where_ref[1], where_ref[2]
    for outer, piece in enumerate((piece0, piece1, piece2, piece3)):
        for inner in range(4):
            far, near = RELATIVE[outer] + 4, RELATIVE[inner] + 4
            if order == 0:
                xx, yy = lax.rem(x + far, 4), lax.rem(y + near, 4)
            else:
                xx, yy = lax.rem(x + near, 4), lax.rem(y + far, 4)
            for k in range(2):
                zz = z if k == 0 else 1 - z
                start = pl.multiple_of((zz * 16 + yy * 4 + xx) * 16, 16)
                x_ref[pl.ds(start, 16), :] = piece[inner, k]
    rows = padded.shape[0]
    clear_margins(padded)

    def chunk(j, carry):
        lanes = pl.ds(pl.multiple_of(j * LANES, LANES), LANES)
        fill_padded(padded, x_ref, lanes)
        for k, dilation in enumerate(DILATIONS):
            for row in range(rows):
                total = jnp.zeros((W16, LANES), F32)
                for tap, source, shift in taps_of_row(row, rows, dilation):
                    weight = w_depth[9 * k + tap : 9 * k + tap + 1, lanes]
                    total = total + weight * padded[source, PAD + shift : PAD + shift + W16, :]
                depth_ref[k, row * W16 : (row + 1) * W16, lanes] = total.astype(BF16)
        return carry

    lax.fori_loop(0, x_ref.shape[1] // LANES, chunk, 0)

    for branch in range(4):
        columns = slice(branch * HID, (branch + 1) * HID)
        if branch == 0:
            pre = dot_nt(x_ref[...], w_plain[...])
        else:
            pre = dot_nt(depth_ref[branch - 1], w_point[branch - 1])
        joined_ref[:, columns] = jnp.maximum(pre + bias[:, columns], 0.0).astype(BF16)
    hidden = jnp.maximum(dot_nt(joined_ref[...], w_proj[...]) + proj_bias[...], 0.0).astype(BF16)
    logits = dot_nt(w_class[...], hidden) + class_bias[...]
    top = jnp.max(logits, axis=0, keepdims=True)
    raised = jnp.exp(logits - top)
    share = raised / jnp.sum(raised, axis=0, keepdims=True)
    class_ids = lax.broadcasted_iota(jnp.int32, logits.shape, 0)
    dlogits = share - jnp.where(class_ids == marks[...], 1.0, 0.0)
    dclass_bias_ref[...] = jnp.broadcast_to(
        jnp.sum(dlogits, axis=1, keepdims=True), dclass_bias_ref.shape
    )
    short = dlogits.astype(BF16)
    dclass_ref[...] = dot_nn(short, hidden)
    dhidden = dot_tn(short, w_class[...])
    dpre = jnp.where(hidden.astype(F32) > 0, dhidden, 0.0)
    dpre_short = dpre.astype(BF16)
    dpre_ref[...] = dpre_short
    sums_ref[...] = jnp.zeros(sums_ref.shape, F32)
    sums_ref[1:2, 0:HID] = jnp.sum(dpre_short.astype(F32), axis=0, keepdims=True)
    for branch in range(4):
        columns = slice(branch * HID, (branch + 1) * HID)
        djoined = dot_nn(dpre_short, w_proj[:, columns])
        dz = jnp.where(joined_ref[:, columns].astype(F32) > 0, djoined, 0.0).astype(BF16)
        dz_ref[:, columns] = dz
        sums_ref[0:1, columns] = jnp.sum(dz.astype(F32), axis=0, keepdims=True)


VMEM = pl.BlockSpec(memory_space=pltpu.VMEM)
SMEM = pl.BlockSpec(memory_space=pltpu.SMEM)


def front(order, where, pieces, marks, weights):
    pixels, channels = marks.shape[1], weights[0].shape[1]
    shapes = (
        ((pixels, channels), BF16),
        ((3, pixels, channels), BF16),
        ((pixels, 4 * HID), BF16),
        ((pixels, HID), BF16),
        ((pixels, 4 * HID), BF16),
        ((8, 4 * HID), F32),
        ((32, HID), F32),
        ((32, LANES), F32),
    )
    return pl.pallas_call(
        functools.partial(front_kernel, order),
        name="front",
        out_shape=[jax.ShapeDtypeStruct(*shape) for shape in shapes],
        in_specs=[SMEM] + [VMEM] * (4 + 1 + len(weights)),
        out_specs=[VMEM] * len(shapes),
        scratch_shapes=[pltpu.VMEM((pixels // W16, 2 * PAD + W16, LANES), F32)],
        compiler_params=pltpu.CompilerParams(vmem_limit_bytes=40 * 2**20),
        cost_estimate=pl.CostEstimate(
            flops=3_000_000_000, bytes_accessed=12_000_000, transcendentals=16384
        ),
    )(where, *pieces, marks, *weights)


def taps_kernel(x_ref, dz_ref, w_point, out_ref, padded, ddepth):
    rows = padded.shape[1]
    halves = x_ref.shape[1] // LANES
    for half in range(halves):
        clear_margins(padded.at[half])
        fill_padded(padded.at[half], x_ref, slice(half * LANES, (half + 1) * LANES))
    out_ref[...] = jnp.zeros(out_ref.shape, F32)
    for k, dilation in enumerate(DILATIONS):
        back = dot_nn(dz_ref[:, (k + 1) * HID : (k + 2) * HID], w_point[k])
        ddepth[k] = back.astype(BF16).astype(F32)
    for half in range(halves):
        lanes = slice(half * LANES, (half + 1) * LANES)
        for k, dilation in enumerate(DILATIONS):
            totals = {}
            for row in range(rows):
                slope = ddepth[k, row * W16 : (row + 1) * W16, lanes]
                for tap, source, shift in taps_of_row(row, rows, dilation):
                    value = slope * padded[half, source, PAD + shift : PAD + shift + W16, :]
                    value = jnp.sum(value.reshape(W16 // 8, 8, LANES), axis=0)
                    totals[tap] = value if tap not in totals else totals[tap] + value
            for tap, value in totals.items():
                out_ref[9 * k + tap : 9 * k + tap + 1, lanes] = jnp.sum(
                    value, axis=0, keepdims=True
                )


def depth_taps(x, dz, w_point):
    pixels, channels = x.shape
    block = 256
    return pl.pallas_call(
        taps_kernel,
        name="taps",
        grid=(channels // block,),
        out_shape=jax.ShapeDtypeStruct((32, channels), F32),
        in_specs=[
            pl.BlockSpec((pixels, block), lambda j: (0, j)),
            pl.BlockSpec(dz.shape, lambda j: (0, 0)),
            pl.BlockSpec((3, HID, block), lambda j: (0, 0, j)),
        ],
        out_specs=pl.BlockSpec((32, block), lambda j: (0, j)),
        scratch_shapes=[
            pltpu.VMEM((block // LANES, pixels // W16, 2 * PAD + W16, LANES), F32),
            pltpu.VMEM((3, pixels, block), F32),
        ],
        compiler_params=pltpu.CompilerParams(vmem_limit_bytes=40 * 2**20),
        cost_estimate=pl.CostEstimate(
            flops=1_500_000_000, bytes_accessed=4_000_000, transcendentals=0
        ),
    )(x, dz, w_point)


def product_kernel(count, *refs):
    out_ref = refs[-1]
    total = None
    for m in range(count):
        right = refs[count + m]
        right = right[0] if len(right.shape) == 3 else right[...]
        part = dot_tn(refs[m][...], right)
        total = part if total is None else total + part
    out_ref[...] = total.astype(BF16).reshape(out_ref.shape)


def products(lefts, first, rights, layers=None):
    pixels, channels = rights[0].shape[-2:]
    count, block = len(lefts), 512
    steps = channels // block
    if layers is None:
        grid, shape = (steps,), (HID, channels)
        left_spec = pl.BlockSpec((pixels, HID), lambda j: (0, first))
        right_spec = pl.BlockSpec((pixels, block), lambda j: (0, j))
        out_spec = pl.BlockSpec((HID, block), lambda j: (0, j))
    else:
        grid, shape = (layers, steps), (layers, HID, channels)
        left_spec = pl.BlockSpec((pixels, HID), lambda k, j: (0, first + k))
        right_spec = pl.BlockSpec((1, pixels, block), lambda k, j: (k, 0, j))
        out_spec = pl.BlockSpec((1, HID, block), lambda k, j: (k, 0, j))
    return pl.pallas_call(
        functools.partial(product_kernel, count),
        name="products",
        grid=grid,
        out_shape=jax.ShapeDtypeStruct(shape, BF16),
        in_specs=[left_spec] * count + [right_spec] * count,
        out_specs=out_spec,
        compiler_params=pltpu.CompilerParams(vmem_limit_bytes=40 * 2**20),
        cost_estimate=pl.CostEstimate(
            flops=(layers or 1) * 1_073_741_824,
            bytes_accessed=(layers or 1) * 5_000_000,
            transcendentals=0,
        ),
    )(*lefts, *rights)


def place(z, y, x):
    return z * 16 + (y % 4) * 4 + x % 4


EVERY = [(z, y, x) for z in range(2) for y in range(4) for x in range(4)]


def along_x(step):
    return [(place(z, y, x), place(z, y, x + step)) for z, y, x in EVERY]


def along_y(step):
    return [(place(z, y, x), place(z, y + step, x)) for z, y, x in EVERY]


ACROSS_Z = [(t, (t + 16) % 32) for t in range(32)]
FLIPS = (
    [(place(z, y, x), place(z, y, x ^ 1)) for z, y, x in EVERY],
    [(place(z, y, x), place(z, y, x ^ 2)) for z, y, x in EVERY],
    [(place(z, y, x), place(z, y ^ 1, x)) for z, y, x in EVERY],
    [(place(z, y, x), place(z, y ^ 2, x)) for z, y, x in EVERY],
    ACROSS_Z,
)
CORES = [(b, b ^ 1) for b in range(4)]
CHIPS = [(b, b ^ 2) for b in range(4)]


def gather_ring(block, along):
    return (
        block,
        lax.ppermute(block, "trial", along(1)),
        lax.ppermute(block, "trial", along(-1)),
        lax.ppermute(block, "trial", along(2)),
    )


def gather_map(block, order):
    inner, outer = (along_y, along_x) if order == 0 else (along_x, along_y)
    return gather_ring(jnp.stack(gather_ring(block, inner)), outer)


def in_order(mine, other, first):
    return jnp.where(first, jnp.stack([mine, other]), jnp.stack([other, mine]))


def gather_batch(mine, core, chip):
    pair = in_order(mine, lax.ppermute(mine, "batch", CORES), core == 0)
    both = in_order(pair, lax.ppermute(pair, "batch", CHIPS), chip == 0)
    return both.reshape((4,) + mine.shape)


def sum_batch(partial, core):
    half = partial.shape[0] // 2
    mine = lax.dynamic_slice_in_dim(partial, core * half, half, 0)
    other = lax.dynamic_slice_in_dim(partial, (1 - core) * half, half, 0)
    pair = mine.astype(F32) + lax.ppermute(other, "batch", CORES).astype(F32)
    pair = pair.astype(BF16)
    total = pair.astype(F32) + lax.ppermute(pair, "batch", CHIPS).astype(F32)
    total = total.astype(BF16)
    rest = lax.ppermute(total, "batch", CORES)
    return in_order(total, rest, core == 0).reshape(partial.shape)


def sum_batch_small(partial):
    pair = partial.astype(F32) + lax.ppermute(partial, "batch", CORES).astype(F32)
    pair = pair.astype(BF16)
    return pair.astype(F32) + lax.ppermute(pair, "batch", CHIPS).astype(F32)


def pick(table, plan):
    return jnp.stack(
        [lax.dynamic_index_in_dim(table, plan[m], 0, keepdims=False) for m in range(plan.shape[0])]
    )


def pool_map(coarse):
    return (jnp.sum(coarse, axis=-1, dtype=F32) / coarse.shape[-1]).astype(BF16)


def on_device(
    features16,
    features32,
    labels,
    plan,
    lr_index,
    w_plain,
    w_depth,
    w_point,
    w_pool,
    b_branch,
    w_proj,
    b_proj,
    w_class,
    b_class,
):
    turns = plan.shape[0]
    trial = lax.axis_index("trial")
    batch = lax.axis_index("batch")
    core, chip = batch % 2, batch // 2
    where = jnp.stack([trial % 4, (trial // 4) % 4, trial // 16]).astype(jnp.int32)

    own = features16[0, 0].T.reshape(32, 16, -1)
    pieces = lax.all_to_all(own, "trial", 0, 0, tiled=True)
    picked = pick(pieces, plan)
    halves = jnp.stack([picked, lax.ppermute(picked, "trial", ACROSS_Z)], axis=1)
    maps = [gather_map(halves[m], m % 2) for m in range(turns)]

    pooled_own = pool_map(features32[0, 0])
    pooled = jnp.where((plan == trial)[:, None], pooled_own[None, :], jnp.zeros((), BF16))
    for flip in FLIPS:
        pooled = pooled + lax.ppermute(pooled, "trial", flip)

    point16 = w_point[0].astype(BF16)
    proj16 = w_proj[0].astype(BF16)
    taps = jnp.pad(w_depth[0].reshape(27, -1), ((0, 5), (0, 0)))
    classes = w_class.shape[1]
    class16 = jnp.pad(w_class[0].astype(BF16), ((0, 32 - classes), (0, 0)))
    class_bias = jnp.pad(b_class[0], (0, 32 - classes), constant_values=-1e30)[:, None]
    wide = 4 * HID
    branch4 = jax.nn.relu(dot_nt(pooled, w_pool[0].astype(BF16)) + b_branch[0, 4]).astype(BF16)
    proj_bias = dot_nt(branch4, proj16[:, wide:]) + b_proj[0]
    marks = pick(labels[:, 0], plan)

    fronts = []
    for m in range(turns):
        weights = (
            w_plain[0].astype(BF16),
            taps,
            point16,
            b_branch[0, :4].reshape(1, wide),
            proj16[:, :wide],
            proj_bias[m : m + 1],
            class16,
            class_bias,
        )
        fronts.append(front(m % 2, where, maps[m], marks[m : m + 1], weights))
    xs, depths, joined, dpres, dzs, sums, dclass, dclass_bias = zip(*fronts)

    proj_grad = sum_batch(products(dpres, 0, joined), core)
    plain_grad = sum_batch(products(dzs, 0, xs), core)
    point_grad = sum_batch(products(dzs, 1, depths, 3).reshape(3 * HID, -1), core)
    depth_part = sum(depth_taps(x, dz, point16) for x, dz in zip(xs, dzs))

    dbias_proj = jnp.stack([part[1, :HID] for part in sums])
    dbranch4 = lax.dot_general(
        dbias_proj,
        proj16[:, wide:].astype(F32),
        (((1,), (0,)), ((), ())),
        precision=lax.Precision.HIGHEST,
        preferred_element_type=F32,
    )
    dbranch4 = jnp.where(branch4 > 0, dbranch4, 0.0)
    slopes = gather_batch(jnp.concatenate([dbranch4, dbias_proj], axis=1), core, chip)
    inputs = gather_batch(jnp.concatenate([pooled, branch4], axis=1), core, chip)
    slopes = slopes.reshape(4 * turns, -1)
    inputs = inputs.reshape(4 * turns, -1).astype(F32)

    def outer(left, right):
        return lax.dot_general(
            left,
            right,
            (((0,), (0,)), ((), ())),
            precision=lax.Precision.HIGHEST,
            preferred_element_type=F32,
        )

    coarse = pooled.shape[1]
    pool_grad = outer(slopes[:, :HID], inputs[:, :coarse])
    proj4_grad = outer(slopes[:, HID:], inputs[:, coarse:])

    small = jnp.concatenate(
        [
            depth_part[:27].reshape(-1),
            sum(part[0] for part in sums),
            jnp.sum(dbranch4, axis=0),
            jnp.sum(dbias_proj, axis=0),
            sum(dclass)[:classes].reshape(-1),
            sum(dclass_bias)[:classes, 0],
        ]
    )
    length = small.shape[0]
    small = jnp.pad(small, (0, -length % 16384)).astype(BF16).reshape(-1, 1024)
    small = sum_batch_small(small).reshape(-1)[:length]
    sizes = (27 * w_depth.shape[-1], 5 * HID, HID, classes * HID, classes)
    cut, start = [], 0
    for size in sizes:
        cut.append(small[start : start + size])
        start += size
    params = (w_plain, w_depth, w_point, w_pool, b_branch, w_proj, b_proj, w_class, b_class)
    grads = (
        plain_grad.astype(F32),
        cut[0],
        point_grad.astype(F32),
        pool_grad,
        cut[1],
        jnp.concatenate([proj_grad.astype(F32), proj4_grad], axis=1),
        cut[2],
        cut[3],
        cut[4],
    )
    squares = sum(jnp.sum(grad * grad) for grad in grads)
    entries = sum(weight.size for weight in params)
    norm_scale = jnp.sqrt(squares / entries + 1e-06)
    step_rate = 0.5 * jnp.exp2(-6.0 * lr_index[0].astype(F32) / 1073741824.0)
    return tuple(
        weight - step_rate * grad.reshape(weight.shape) / norm_scale
        for weight, grad in zip(params, grads)
    )


def solution(mesh):
    in_specs = (
        P("trial", "batch", None, None),
        P("trial", "batch", None, None),
        P(None, "batch", None),
        P(),
        P("trial"),
        P("trial", None, None),
        P("trial", None, None, None),
        P("trial", None, None, None),
        P("trial", None, None),
        P("trial", None, None),
        P("trial", None, None),
        P("trial", None),
        P("trial", None, None),
        P("trial", None),
    )
    out_specs = (
        P("trial", None, None),
        P("trial", None, None, None),
        P("trial", None, None, None),
        P("trial", None, None),
        P("trial", None, None),
        P("trial", None, None),
        P("trial", None),
        P("trial", None, None),
        P("trial", None),
    )
    return jax.shard_map(
        on_device, mesh=mesh, in_specs=in_specs, out_specs=out_specs, check_vma=False
    )
```

```python
import functools

import jax
import jax.numpy as jnp
from jax import lax
from jax.experimental import pallas as pl
from jax.experimental.pallas import tpu as pltpu
from jax.sharding import PartitionSpec as P

W16 = 32
HID = 256
PAD = 24
DILATIONS = (6, 12, 18)
LANES = 128
RELATIVE = (0, -1, 1, 2)
BF16 = jnp.bfloat16
F32 = jnp.float32


def dot_nt(a, b):
    return lax.dot_general(a, b, (((1,), (1,)), ((), ())), preferred_element_type=F32)


def dot_nn(a, b):
    return lax.dot_general(a, b, (((1,), (0,)), ((), ())), preferred_element_type=F32)


def dot_exact(a, b):
    return lax.dot_general(
        a,
        b,
        (((1,), (0,)), ((), ())),
        precision=lax.Precision.HIGHEST,
        preferred_element_type=F32,
    )


def dot_exact_nt(a, b):
    return lax.dot_general(
        a,
        b,
        (((1,), (1,)), ((), ())),
        precision=lax.Precision.HIGHEST,
        preferred_element_type=F32,
    )


def dot_tn(a, b):
    return lax.dot_general(a, b, (((0,), (0,)), ((), ())), preferred_element_type=F32)


def taps_of_row(row, rows, dilation):
    taps = []
    for a in (-1, 0, 1):
        source = row + a * dilation
        if 0 <= source < rows:
            for b in (-1, 0, 1):
                taps.append((3 * (a + 1) + (b + 1), source, b * dilation))
    return taps


def clear_margins(padded):
    rows = padded.shape[0]
    blank = jnp.zeros((rows, PAD, LANES), F32)
    padded[:, 0:PAD, :] = blank
    padded[:, PAD + W16 : 2 * PAD + W16, :] = blank


def fill_padded(padded, x_ref, lanes):
    for row in range(padded.shape[0]):
        padded[row, PAD : PAD + W16, :] = x_ref[row * W16 : (row + 1) * W16, lanes].astype(F32)


def front_kernel(
    order,
    where_ref,
    piece0,
    piece1,
    piece2,
    piece3,
    marks,
    w_plain,
    w_depth,
    w_point,
    bias,
    w_proj,
    proj_bias,
    w_class,
    class_bias,
    maps_ref,
    joined_ref,
    dpre_ref,
    dz_ref,
    sums_ref,
    dclass_ref,
    padded,
):
    x_ref = maps_ref.at[0]
    x, y, z = where_ref[0], where_ref[1], where_ref[2]
    for outer, piece in enumerate((piece0, piece1, piece2, piece3)):
        for inner in range(4):
            far, near = RELATIVE[outer] + 4, RELATIVE[inner] + 4
            if order == 0:
                xx, yy = lax.rem(x + far, 4), lax.rem(y + near, 4)
            else:
                xx, yy = lax.rem(x + near, 4), lax.rem(y + far, 4)
            for k in range(2):
                zz = z if k == 0 else 1 - z
                start = pl.multiple_of((zz * 16 + yy * 4 + xx) * 16, 16)
                x_ref[pl.ds(start, 16), :] = piece[pl.ds((2 * inner + k) * 16, 16), :]
    rows = padded.shape[0]
    clear_margins(padded)

    def chunk(j, carry):
        lanes = pl.ds(pl.multiple_of(j * LANES, LANES), LANES)
        fill_padded(padded, x_ref, lanes)
        for k, dilation in enumerate(DILATIONS):
            for row in range(rows):
                total = jnp.zeros((W16, LANES), F32)
                for tap, source, shift in taps_of_row(row, rows, dilation):
                    weight = w_depth[9 * k + tap, :, lanes]
                    total = total + weight * padded[source, PAD + shift : PAD + shift + W16, :]
                maps_ref[k + 1, row * W16 : (row + 1) * W16, lanes] = total.astype(BF16)
        return carry

    lax.fori_loop(0, x_ref.shape[1] // LANES, chunk, 0)

    for branch in range(4):
        columns = slice(branch * HID, (branch + 1) * HID)
        if branch == 0:
            pre = dot_nt(x_ref[...], w_plain[...])
        else:
            pre = dot_nt(maps_ref[branch], w_point[branch - 1])
        joined_ref[:, columns] = jnp.maximum(pre + bias[:, columns], 0.0).astype(BF16)
    hidden = jnp.maximum(dot_nt(joined_ref[...], w_proj[...]) + proj_bias[...], 0.0).astype(BF16)
    logits = dot_nt(w_class[...], hidden) + class_bias[...]
    top = jnp.max(logits, axis=0, keepdims=True)
    raised = jnp.exp(logits - top)
    share = raised / jnp.sum(raised, axis=0, keepdims=True)
    class_ids = lax.broadcasted_iota(jnp.int32, logits.shape, 0)
    dlogits = share - jnp.where(class_ids == marks[...], 1.0, 0.0)
    square = (logits.shape[0], LANES)
    column = jnp.broadcast_to(jnp.sum(dlogits, axis=1, keepdims=True), square)
    on_diagonal = lax.broadcasted_iota(jnp.int32, square, 0) == lax.broadcasted_iota(
        jnp.int32, square, 1
    )
    short = dlogits.astype(BF16)
    dclass_ref[...] = dot_nn(short, hidden)
    dhidden = dot_tn(short, w_class[...])
    dpre = jnp.where(hidden.astype(F32) > 0, dhidden, 0.0)
    dpre_short = dpre.astype(BF16)
    dpre_ref[...] = dpre_short
    sums_ref[...] = jnp.zeros(sums_ref.shape, F32)
    sums_ref[3:4, 0:LANES] = jnp.sum(jnp.where(on_diagonal, column, 0.0), axis=0, keepdims=True)
    sums_ref[1:2, 0:HID] = jnp.sum(dpre_short.astype(F32), axis=0, keepdims=True)
    for branch in range(4):
        columns = slice(branch * HID, (branch + 1) * HID)
        djoined = dot_nn(dpre_short, w_proj[:, columns])
        dz = jnp.where(joined_ref[:, columns].astype(F32) > 0, djoined, 0.0).astype(BF16)
        dz_ref[:, columns] = dz
        sums_ref[0:1, columns] = jnp.sum(dz.astype(F32), axis=0, keepdims=True)


VMEM = pl.BlockSpec(memory_space=pltpu.VMEM)
SMEM = pl.BlockSpec(memory_space=pltpu.SMEM)


def front(order, where, pieces, marks, weights):
    pixels, channels = marks.shape[1], weights[0].shape[1]
    shapes = (
        ((4, pixels, channels), BF16),
        ((pixels, 4 * HID), BF16),
        ((pixels, HID), BF16),
        ((pixels, 4 * HID), BF16),
        ((8, 4 * HID), F32),
        ((32, HID), F32),
    )
    return pl.pallas_call(
        functools.partial(front_kernel, order),
        name="front",
        out_shape=[pltpu.VMEM(*shape) for shape in shapes],
        in_specs=[SMEM] + [VMEM] * (4 + 1 + len(weights)),
        out_specs=[VMEM] * len(shapes),
        scratch_shapes=[pltpu.VMEM((pixels // W16, 2 * PAD + W16, LANES), F32)],
        compiler_params=pltpu.CompilerParams(vmem_limit_bytes=16 * 2**20),
        cost_estimate=pl.CostEstimate(
            flops=6_700_000_000, bytes_accessed=12_000_000, transcendentals=16384
        ),
    )(where, *pieces, marks, *weights)


def taps_kernel(maps_ref, dz_ref, w_point, out_ref, padded, ddepth):
    x_ref = maps_ref.at[0]
    rows = padded.shape[1]
    halves = padded.shape[0]
    for half in range(halves):
        start = pl.multiple_of((pl.program_id(0) * halves + half) * LANES, LANES)
        clear_margins(padded.at[half])
        fill_padded(padded.at[half], x_ref, pl.ds(start, LANES))
    out_ref[...] = jnp.zeros(out_ref.shape, F32)
    for k, dilation in enumerate(DILATIONS):
        back = dot_nn(dz_ref[:, (k + 1) * HID : (k + 2) * HID], w_point[k])
        ddepth[k] = back.astype(BF16).astype(F32)
    for half in range(halves):
        lanes = slice(half * LANES, (half + 1) * LANES)
        for k, dilation in enumerate(DILATIONS):
            totals = {}
            for row in range(rows):
                slope = ddepth[k, row * W16 : (row + 1) * W16, lanes]
                for tap, source, shift in taps_of_row(row, rows, dilation):
                    value = slope * padded[half, source, PAD + shift : PAD + shift + W16, :]
                    value = jnp.sum(value.reshape(W16 // 8, 8, LANES), axis=0)
                    totals[tap] = value if tap not in totals else totals[tap] + value
            for tap, value in totals.items():
                out_ref[9 * k + tap : 9 * k + tap + 1, lanes] = jnp.sum(
                    value, axis=0, keepdims=True
                )


def depth_taps(maps, dz, w_point):
    pixels, channels = maps.shape[1:]
    block = 256
    return pl.pallas_call(
        taps_kernel,
        name="taps",
        grid=(channels // block,),
        out_shape=jax.ShapeDtypeStruct((32, channels), F32),
        in_specs=[
            VMEM,
            VMEM,
            pl.BlockSpec((3, HID, block), lambda j: (0, 0, j)),
        ],
        out_specs=pl.BlockSpec((32, block), lambda j: (0, j)),
        scratch_shapes=[
            pltpu.VMEM((block // LANES, pixels // W16, 2 * PAD + W16, LANES), F32),
            pltpu.VMEM((3, pixels, block), F32),
        ],
        compiler_params=pltpu.CompilerParams(vmem_limit_bytes=16 * 2**20),
        cost_estimate=pl.CostEstimate(
            flops=4_500_000_000, bytes_accessed=4_000_000, transcendentals=0
        ),
    )(maps, dz, w_point)


PRODUCT_COLUMNS = 512


def product_kernel(count, first, *refs):
    out_ref = refs[-1]
    layer, step = first + pl.program_id(0), pl.program_id(1)
    left_columns = pl.ds(pl.multiple_of(layer * HID, HID), HID)
    columns = pl.ds(pl.multiple_of(step * PRODUCT_COLUMNS, PRODUCT_COLUMNS), PRODUCT_COLUMNS)
    total = None
    for left, right in zip(refs[:count], refs[count : 2 * count]):
        right = right[layer, :, columns] if len(right.shape) == 3 else right[:, columns]
        part = dot_tn(left[:, left_columns], right)
        total = part if total is None else total + part
    out_ref[0] = total.astype(BF16)


def products(lefts, rights, first, layers):
    channels = rights[0].shape[-1]
    count = len(lefts)
    return pl.pallas_call(
        functools.partial(product_kernel, count, first),
        name="products",
        grid=(layers, channels // PRODUCT_COLUMNS),
        out_shape=jax.ShapeDtypeStruct((layers, HID, channels), BF16),
        in_specs=[VMEM] * (2 * count),
        out_specs=pl.BlockSpec((1, HID, PRODUCT_COLUMNS), lambda k, j: (k, 0, j)),
        compiler_params=pltpu.CompilerParams(vmem_limit_bytes=10 * 2**20),
        cost_estimate=pl.CostEstimate(
            flops=layers * 2_200_000_000, bytes_accessed=layers * 5_000_000, transcendentals=0
        ),
    )(*lefts, *rights)


STEPS = 4


def update_kernel(
    core_ref,
    rate_ref,
    w_plain,
    w_point,
    w_pool,
    w_proj,
    w_depth,
    b_branch,
    b_proj,
    w_class,
    b_class,
    mine0,
    rest0,
    mine1,
    rest1,
    mine2,
    rest2,
    left,
    factors,
    small,
    new_plain,
    new_point,
    new_pool,
    new_proj,
    new_depth,
    new_b_branch,
    new_b_proj,
    new_class,
    new_b_class,
    scale_ref,
):
    step = pl.program_id(0)
    pairs = ((mine0, rest0), (mine1, rest1), (mine2, rest2))
    count = factors.shape[0]
    entries = sum(
        STEPS * array[...].size for array in (w_plain, w_point, w_pool, w_proj)
    ) + sum(array[...].size for array in (w_depth, b_branch, b_proj, w_class, b_class))

    def outer_squared(a, b):
        product = dot_exact_nt(a, a) * dot_exact_nt(b, b)
        return jnp.sum(product, keepdims=True)

    @pl.when(step == 0)
    def _():
        total = jnp.zeros((16, small.shape[1]), F32)
        for mine, rest in pairs:
            for row in range(0, mine.shape[1], 16):
                for layer in range(mine.shape[0]):
                    one = mine[layer, row : row + 16, :].astype(F32)
                    other = rest[layer, row : row + 16, :].astype(F32)
                    total = total + (one * one + other * other)
        for row in range(0, small.shape[0], 16):
            total = total + jnp.square(small[row : row + 16, :])
        squares = jnp.sum(total, keepdims=True)
        squares = squares + outer_squared(factors[:, :HID], factors[:, 3 * HID :])
        squares = squares + outer_squared(
            factors[:, HID : 2 * HID], factors[:, 2 * HID : 3 * HID]
        )
        norm_scale = jnp.sqrt(squares / entries + 1e-06)
        scale_ref[...] = jnp.broadcast_to(rate_ref[0] / norm_scale, scale_ref.shape)

    scale = scale_ref[0:1, 0:1]

    def large(side):
        rows = w_plain.shape[1]
        here = pl.ds(pl.multiple_of(lax.rem(step, STEPS // 2) * rows, rows), rows)
        proj, low, high = (
            [pair[side][layer, here, :] for layer in range(pair[side].shape[0])] for pair in pairs
        )
        wide = proj[0].shape[-1]
        new_plain[0] = w_plain[0] - scale * low[0].astype(F32)
        new_point[0, 0] = w_point[0, 0] - scale * low[1].astype(F32)
        new_point[0, 1] = w_point[0, 1] - scale * high[0].astype(F32)
        new_point[0, 2] = w_point[0, 2] - scale * high[1].astype(F32)
        new_proj[0, :, :wide] = w_proj[0, :, :wide] - scale * proj[0].astype(F32)
        proj4_grad = dot_exact(left[1, :, :count], factors[:, 2 * HID : 3 * HID])
        new_proj[0, :, wide:] = w_proj[0, :, wide:] - scale * proj4_grad
        pool_grad = dot_exact(left[0, :, :count], factors[:, 3 * HID :])
        new_pool[0] = w_pool[0] - scale * pool_grad

    @pl.when(step < STEPS // 2)
    def _():
        large(0)

    @pl.when(step >= STEPS // 2)
    def _():
        large(1)

    @pl.when(step == 0)
    def _():
        for row in range(w_depth.shape[0]):
            new_depth[row] = w_depth[row] - scale * small[row : row + 1, :]
        for branch in range(5):
            row = 32 if branch < 4 else 34
            first = branch % 4 * HID
            new_b_branch[branch] = (
                b_branch[branch] - scale * small[row : row + 1, first : first + HID]
            )
        new_b_proj[...] = b_proj[...] - scale * small[33:34, :HID]
        classes = w_class.shape[0]
        for index in range(classes):
            row, first = 40 + index % 8, index // 8 * HID
            new_class[index] = w_class[index] - scale * small[row : row + 1, first : first + HID]
        new_b_class[...] = b_class[...] - scale * small[35:36, :classes]


def update(core, rate, params, halves, left, factors, small):
    w_plain, w_depth, w_point, w_pool, b_branch, w_proj, b_proj, w_class, b_class = params
    inputs = (w_plain, w_point, w_pool, w_proj) + tuple(
        array if array.ndim == 2 else array.reshape(-1, 1, array.shape[-1])
        for array in (w_depth, b_branch, b_proj, w_class, b_class)
    )
    rows, half = HID // STEPS, STEPS // 2

    def where(step, core_ref):
        return lax.rem(step + core_ref[0] * half, STEPS)

    def by_rows(shape):
        if len(shape) == 2:
            return pl.BlockSpec((rows, shape[1]), lambda j, core: (where(j, core), 0))
        if len(shape) == 3:
            return pl.BlockSpec((1, rows, shape[2]), lambda j, core: (0, where(j, core), 0))
        return pl.BlockSpec((1, shape[1], rows, shape[3]), lambda j, core: (0, 0, where(j, core), 0))

    def whole(shape):
        return pl.BlockSpec(shape, lambda j, core: (0,) * len(shape))

    specs = [by_rows(array.shape) for array in inputs[:4]] + [whole(array.shape) for array in inputs[4:]]
    new = pl.pallas_call(
        update_kernel,
        name="update",
        out_shape=[jax.ShapeDtypeStruct(array.shape, F32) for array in inputs],
        grid_spec=pltpu.PrefetchScalarGridSpec(
            num_scalar_prefetch=1,
            grid=(STEPS,),
            in_specs=[SMEM]
            + specs
            + [VMEM] * (2 * len(halves))
            + [pl.BlockSpec((2, rows, LANES), lambda j, core: (0, where(j, core), 0)), VMEM, VMEM],
            out_specs=specs,
            scratch_shapes=[pltpu.VMEM((8, LANES), F32)],
        ),
        compiler_params=pltpu.CompilerParams(vmem_limit_bytes=60 * 2**20),
        cost_estimate=pl.CostEstimate(
            flops=4_000_000, bytes_accessed=20_000_000, transcendentals=0
        ),
    )(core, rate, *inputs, *(array for pair in halves for array in pair), left, factors, small)
    order = (0, 4, 1, 2, 5, 3, 6, 7, 8)
    return tuple(new[i].reshape(param.shape) for i, param in zip(order, params))


def place(z, y, x):
    return z * 16 + (y % 4) * 4 + x % 4


EVERY = [(z, y, x) for z in range(2) for y in range(4) for x in range(4)]


def along_x(step):
    return [(place(z, y, x), place(z, y, x + step)) for z, y, x in EVERY]


def along_y(step):
    return [(place(z, y, x), place(z, y + step, x)) for z, y, x in EVERY]


ACROSS_Z = [(t, (t + 16) % 32) for t in range(32)]
CORES = [(b, b ^ 1) for b in range(4)]
CHIPS = [(b, b ^ 2) for b in range(4)]


def gather_ring(block, along):
    return (
        block,
        lax.ppermute(block, "trial", along(1)),
        lax.ppermute(block, "trial", along(-1)),
        lax.ppermute(block, "trial", along(2)),
    )


def from_batch(mine):
    return [mine] + [
        lax.ppermute(mine, "batch", [(b, b ^ other) for b in range(4)]) for other in (1, 2, 3)
    ]


def in_order(parts, core, chip):
    near, beside, across, beyond = parts
    low = jnp.where(core == 0, jnp.concatenate([near, beside]), jnp.concatenate([beside, near]))
    high = jnp.where(core == 0, jnp.concatenate([across, beyond]), jnp.concatenate([beyond, across]))
    return jnp.where(chip == 0, jnp.concatenate([low, high]), jnp.concatenate([high, low]))


def sum_cores(partial, core):
    half = partial.shape[1] // 2
    mine = lax.dynamic_slice_in_dim(partial, core * half, half, 1)
    other = lax.dynamic_slice_in_dim(partial, (1 - core) * half, half, 1)
    return (mine.astype(F32) + lax.ppermute(other, "batch", CORES).astype(F32)).astype(BF16)


def sum_chips(pair):
    return (pair.astype(F32) + lax.ppermute(pair, "batch", CHIPS).astype(F32)).astype(BF16)


def sum_batch_small(partial):
    near, beside, across, beyond = [part.astype(F32) for part in from_batch(partial)]
    return (near + beside) + (across + beyond)


def pick(table, plan, turn_ids):
    return jnp.stack(
        [lax.dynamic_index_in_dim(table, plan[m], 0, keepdims=False) for m in turn_ids]
    )


def pool_map(coarse):
    return (jnp.sum(coarse, axis=-1, dtype=F32) / coarse.shape[-1]).astype(BF16)


def on_device(
    features16,
    features32,
    labels,
    plan,
    lr_index,
    w_plain,
    w_depth,
    w_point,
    w_pool,
    b_branch,
    w_proj,
    b_proj,
    w_class,
    b_class,
):
    turns = plan.shape[0]
    trial = lax.axis_index("trial")
    batch = lax.axis_index("batch")
    core, chip = batch % 2, batch // 2
    where = jnp.stack([trial % 4, (trial // 4) % 4, trial // 16]).astype(jnp.int32)

    own = features16[0, 0].T
    channels = own.shape[1]
    pieces = lax.all_to_all(own.reshape(32, 16, channels), "trial", 0, 0, tiled=True)
    turn_lists = [list(range(order, turns, 2)) for order in range(2)]
    picked = pick(pieces, plan, turn_lists[0] + turn_lists[1])
    pooled = pool_map(features32[0, 0]).reshape(-1, 1, channels)
    pooled = jnp.where((plan == trial)[None, :, None], pooled, jnp.zeros((), BF16))
    pooled = pooled.reshape(-1, channels)
    rows = pooled.shape[0]
    across = lax.ppermute(
        jnp.concatenate([picked.reshape(-1, channels), pooled]), "trial", ACROSS_Z
    )
    pooled = pooled + across[-rows:]
    across = across[:-rows].reshape(picked.shape)
    blocks, outers = [None] * turns, [None] * turns
    for order, (inner, outer) in enumerate(((along_y, along_x), (along_x, along_y))):
        turn_ids = turn_lists[order]
        count = len(turn_ids)
        some = slice(order * len(turn_lists[0]), order * len(turn_lists[0]) + count)
        block = jnp.stack([picked[some], across[some]], axis=1).reshape(-1, channels)
        size = block.shape[0]
        if order == 0:
            block = jnp.concatenate([block, pooled])
        ring = gather_ring(block, inner)
        if order == 0:
            pooled = sum(part[size:] for part in ring)
        for place_in, m in enumerate(turn_ids):
            first, last = place_in * size // count, (place_in + 1) * size // count
            parts = [part[first:last] for part in ring]
            blocks[m] = jnp.concatenate(parts + [pooled] if m == 0 else parts)
            outers[m] = outer
    after = lax.optimization_barrier
    maps = [gather_ring(blocks[m], outers[m]) for m in range(2)]
    pooled = sum(part[4 * size // count :] for part in maps[0])
    pooled = [pooled[first : first + turns] for first in range(0, rows, turns)]

    point16 = w_point[0].astype(BF16)
    proj16 = w_proj[0].astype(BF16)
    taps = w_depth.reshape(27, 1, -1)
    classes = w_class.shape[1]
    class16 = jnp.pad(w_class[0].astype(BF16), ((0, 32 - classes), (0, 0)))
    class_bias = jnp.pad(b_class[0], (0, 32 - classes), constant_values=-1e30)[:, None]
    wide = 4 * HID
    pool16 = w_pool[0].astype(BF16)
    branch4 = sum(
        dot_nt(part, pool16[:, i * channels : (i + 1) * channels]) for i, part in enumerate(pooled)
    )
    branch4 = jax.nn.relu(branch4 + b_branch[0, 4]).astype(BF16)
    proj_bias = dot_nt(branch4, proj16[:, wide:]) + b_proj[0]
    marks = pick(labels[:, 0], plan, range(turns))

    fronts = []
    for m in range(turns):
        if m >= 2:
            maps.append(gather_ring(blocks[m], outers[m]))
        weights = (
            w_plain[0].astype(BF16),
            taps,
            point16,
            b_branch[0, :4].reshape(1, wide),
            proj16[:, :wide],
            proj_bias[m : m + 1],
            class16,
            class_bias,
        )
        if m == 0:
            maps[0], blocks[2] = after((maps[0], blocks[2]))
        fronts.append(front(m % 2, where, maps[m], marks[m : m + 1], weights))
        if m == 0:
            fronts[0], maps[1], blocks[3] = after((fronts[0], maps[1], blocks[3]))
    stacks, joined, dpres, dzs, sums, dclass = zip(*fronts)

    dbias_proj = jnp.stack([part[1, :HID] for part in sums])
    dbranch4 = dot_exact(dbias_proj, proj16[:, wide:].astype(F32))
    dbranch4 = jnp.where(branch4 > 0, dbranch4, 0.0)
    factors = [dbranch4, dbias_proj, branch4] + pooled
    factors = jnp.concatenate([part.astype(F32) for part in factors], axis=1)
    factors = from_batch(jnp.pad(factors, ((0, 8 - turns), (0, 0))))
    proj_part = products(dpres, joined, 0, 1)
    dzs, proj_part = after((dzs, proj_part))
    proj_pair = sum_cores(proj_part, core)
    low_part = products(dzs, stacks, 0, 2)
    dzs, low_part, proj_pair = after((dzs, low_part, proj_pair))
    low_pair = sum_cores(low_part, core)
    high_part = products(dzs, stacks, 2, 2)
    proj_total = sum_chips(proj_pair)
    dzs, high_part, low_pair = after((dzs, high_part, low_pair))
    high_pair = sum_cores(high_part, core)
    depth_part = depth_taps(stacks[0], dzs[0], point16)
    dzs, depth_part, high_pair, proj_total = after((dzs, depth_part, high_pair, proj_total))
    low_total = sum_chips(low_pair)
    for m in range(1, turns):
        depth_part = depth_part + depth_taps(stacks[m], dzs[m], point16)
        if m == 2:
            low_total, depth_part = after((low_total, depth_part))
    totals = [proj_total, low_total, sum_chips(high_pair)]
    halves = [(total, lax.ppermute(total, "batch", CORES)) for total in totals]

    factors, depth_part = after((factors, depth_part))
    factors = in_order(factors, core, chip)
    left = jnp.pad(factors[:, : 2 * HID].T, ((0, 0), (0, LANES - factors.shape[0])))
    left = left.reshape(2, HID, LANES)

    dclass = sum(dclass)
    bias_row = jnp.pad(jnp.sum(dbranch4, axis=0)[None], ((2, 5), (0, wide - HID)))
    small = jnp.concatenate(
        [
            depth_part,
            sum(sums) + bias_row,
            jnp.concatenate([dclass[8 * g : 8 * g + 8] for g in range(4)], axis=1),
        ]
    )
    small = sum_batch_small(small.astype(BF16))

    params = (w_plain, w_depth, w_point, w_pool, b_branch, w_proj, b_proj, w_class, b_class)

    step_rate = 0.5 * jnp.exp2(-6.0 * lr_index[0].astype(F32) / 1073741824.0)
    return update(
        core.reshape(1).astype(jnp.int32), step_rate.reshape(1), params, halves, left, factors, small
    )


def solution(mesh):
    in_specs = (
        P("trial", "batch", None, None),
        P("trial", "batch", None, None),
        P(None, "batch", None),
        P(),
        P("trial"),
        P("trial", None, None),
        P("trial", None, None, None),
        P("trial", None, None, None),
        P("trial", None, None),
        P("trial", None, None),
        P("trial", None, None),
        P("trial", None),
        P("trial", None, None),
        P("trial", None),
    )
    out_specs = (
        P("trial", None, None),
        P("trial", None, None, None),
        P("trial", None, None, None),
        P("trial", None, None),
        P("trial", None, None),
        P("trial", None, None),
        P("trial", None),
        P("trial", None, None),
        P("trial", None),
    )
    return jax.shard_map(
        on_device, mesh=mesh, in_specs=in_specs, out_specs=out_specs, check_vma=False
    )
```

```python
import functools
import math

import jax
import jax.numpy as jnp
from jax import lax
from jax.experimental import pallas as pl
from jax.experimental.pallas import tpu as pltpu
from jax.sharding import PartitionSpec as P

W16 = 32
HID = 256
PAD = 24
DILATIONS = (6, 12, 18)
LANES = 128
RELATIVE = (0, -1, 1, 2)
BF16 = jnp.bfloat16
F32 = jnp.float32


def dot_nt(a, b):
    return lax.dot_general(a, b, (((1,), (1,)), ((), ())), preferred_element_type=F32)


def dot_nn(a, b):
    return lax.dot_general(a, b, (((1,), (0,)), ((), ())), preferred_element_type=F32)


def dot_exact(a, b):
    return lax.dot_general(
        a,
        b,
        (((1,), (0,)), ((), ())),
        precision=lax.Precision.HIGHEST,
        preferred_element_type=F32,
    )


def dot_exact_nt(a, b):
    return lax.dot_general(
        a,
        b,
        (((1,), (1,)), ((), ())),
        precision=lax.Precision.HIGHEST,
        preferred_element_type=F32,
    )


def dot_tn(a, b):
    return lax.dot_general(a, b, (((0,), (0,)), ((), ())), preferred_element_type=F32)


def taps_of_row(row, rows, dilation):
    taps = []
    for a in (-1, 0, 1):
        source = row + a * dilation
        if 0 <= source < rows:
            for b in (-1, 0, 1):
                taps.append((3 * (a + 1) + (b + 1), source, b * dilation))
    return taps


def clear_margins(padded):
    rows = padded.shape[0]
    blank = jnp.zeros((rows, PAD, LANES), F32)
    padded[:, 0:PAD, :] = blank
    padded[:, PAD + W16 : 2 * PAD + W16, :] = blank


def fill_padded(padded, x_ref, lanes):
    for row in range(padded.shape[0]):
        padded[row, PAD : PAD + W16, :] = x_ref[row * W16 : (row + 1) * W16, lanes].astype(F32)


def front_kernel(
    order,
    where_ref,
    piece0,
    piece1,
    piece2,
    piece3,
    marks,
    w_plain,
    w_depth,
    w_point,
    bias,
    w_proj,
    proj_bias,
    w_class,
    class_bias,
    maps_ref,
    joined_ref,
    dpre_ref,
    dz_ref,
    sums_ref,
    dclass_ref,
    padded,
):
    x_ref = maps_ref.at[0]
    x, y, z = where_ref[0], where_ref[1], where_ref[2]
    for outer, piece in enumerate((piece0, piece1, piece2, piece3)):
        for inner in range(4):
            far, near = RELATIVE[outer] + 4, RELATIVE[inner] + 4
            if order == 0:
                xx, yy = lax.rem(x + far, 4), lax.rem(y + near, 4)
            else:
                xx, yy = lax.rem(x + near, 4), lax.rem(y + far, 4)
            for k in range(2):
                zz = z if k == 0 else 1 - z
                start = pl.multiple_of((zz * 16 + yy * 4 + xx) * 16, 16)
                x_ref[pl.ds(start, 16), :] = piece[pl.ds((2 * inner + k) * 16, 16), :]
    rows = padded.shape[0]
    clear_margins(padded)

    def chunk(j, carry):
        lanes = pl.ds(pl.multiple_of(j * LANES, LANES), LANES)
        fill_padded(padded, x_ref, lanes)
        for k, dilation in enumerate(DILATIONS):
            for row in range(rows):
                total = jnp.zeros((W16, LANES), F32)
                for tap, source, shift in taps_of_row(row, rows, dilation):
                    weight = w_depth[9 * k + tap, :, lanes]
                    total = total + weight * padded[source, PAD + shift : PAD + shift + W16, :]
                maps_ref[k + 1, row * W16 : (row + 1) * W16, lanes] = total.astype(BF16)
        return carry

    lax.fori_loop(0, x_ref.shape[1] // LANES, chunk, 0)

    for branch in range(4):
        columns = slice(branch * HID, (branch + 1) * HID)
        if branch == 0:
            pre = dot_nt(x_ref[...], w_plain[...])
        else:
            pre = dot_nt(maps_ref[branch], w_point[branch - 1])
        joined_ref[:, columns] = jnp.maximum(pre + bias[:, columns], 0.0).astype(BF16)
    hidden = jnp.maximum(dot_nt(joined_ref[...], w_proj[...]) + proj_bias[...], 0.0).astype(BF16)
    logits = dot_nt(w_class[...], hidden) + class_bias[...]
    top = jnp.max(logits, axis=0, keepdims=True)
    raised = jnp.exp(logits - top)
    share = raised / jnp.sum(raised, axis=0, keepdims=True)
    class_ids = lax.broadcasted_iota(jnp.int32, logits.shape, 0)
    dlogits = share - jnp.where(class_ids == marks[...], 1.0, 0.0)
    square = (logits.shape[0], LANES)
    column = jnp.broadcast_to(jnp.sum(dlogits, axis=1, keepdims=True), square)
    on_diagonal = lax.broadcasted_iota(jnp.int32, square, 0) == lax.broadcasted_iota(
        jnp.int32, square, 1
    )
    short = dlogits.astype(BF16)
    dclass_ref[...] = dot_nn(short, hidden)
    dhidden = dot_tn(short, w_class[...])
    dpre = jnp.where(hidden.astype(F32) > 0, dhidden, 0.0)
    dpre_short = dpre.astype(BF16)
    dpre_ref[...] = dpre_short
    sums_ref[...] = jnp.zeros(sums_ref.shape, F32)
    sums_ref[3:4, 0:LANES] = jnp.sum(jnp.where(on_diagonal, column, 0.0), axis=0, keepdims=True)
    sums_ref[1:2, 0:HID] = jnp.sum(dpre_short.astype(F32), axis=0, keepdims=True)
    for branch in range(4):
        columns = slice(branch * HID, (branch + 1) * HID)
        djoined = dot_nn(dpre_short, w_proj[:, columns])
        dz = jnp.where(joined_ref[:, columns].astype(F32) > 0, djoined, 0.0).astype(BF16)
        dz_ref[:, columns] = dz
        sums_ref[0:1, columns] = jnp.sum(dz.astype(F32), axis=0, keepdims=True)


VMEM = pl.BlockSpec(memory_space=pltpu.VMEM)
SMEM = pl.BlockSpec(memory_space=pltpu.SMEM)


def front(order, where, pieces, marks, weights):
    pixels, channels = marks.shape[1], weights[0].shape[1]
    shapes = (
        ((4, pixels, channels), BF16),
        ((pixels, 4 * HID), BF16),
        ((pixels, HID), BF16),
        ((pixels, 4 * HID), BF16),
        ((8, 4 * HID), F32),
        ((32, HID), F32),
    )
    return pl.pallas_call(
        functools.partial(front_kernel, order),
        name="front",
        out_shape=[pltpu.VMEM(*shape) for shape in shapes],
        in_specs=[SMEM] + [VMEM] * (4 + 1 + len(weights)),
        out_specs=[VMEM] * len(shapes),
        scratch_shapes=[pltpu.VMEM((pixels // W16, 2 * PAD + W16, LANES), F32)],
        compiler_params=pltpu.CompilerParams(vmem_limit_bytes=16 * 2**20),
        cost_estimate=pl.CostEstimate(
            flops=6_700_000_000, bytes_accessed=12_000_000, transcendentals=16384
        ),
    )(where, *pieces, marks, *weights)


def taps_kernel(maps_ref, dz_ref, w_point, out_ref, padded, ddepth):
    x_ref = maps_ref.at[0]
    rows = padded.shape[1]
    halves = padded.shape[0]
    for half in range(halves):
        start = pl.multiple_of((pl.program_id(0) * halves + half) * LANES, LANES)
        clear_margins(padded.at[half])
        fill_padded(padded.at[half], x_ref, pl.ds(start, LANES))
    out_ref[...] = jnp.zeros(out_ref.shape, F32)
    for k, dilation in enumerate(DILATIONS):
        back = dot_nn(dz_ref[:, (k + 1) * HID : (k + 2) * HID], w_point[k])
        ddepth[k] = back.astype(BF16).astype(F32)
    for half in range(halves):
        lanes = slice(half * LANES, (half + 1) * LANES)
        for k, dilation in enumerate(DILATIONS):
            totals = {}
            for row in range(rows):
                slope = ddepth[k, row * W16 : (row + 1) * W16, lanes]
                for tap, source, shift in taps_of_row(row, rows, dilation):
                    value = slope * padded[half, source, PAD + shift : PAD + shift + W16, :]
                    value = jnp.sum(value.reshape(W16 // 8, 8, LANES), axis=0)
                    totals[tap] = value if tap not in totals else totals[tap] + value
            for tap, value in totals.items():
                out_ref[9 * k + tap : 9 * k + tap + 1, lanes] = jnp.sum(
                    value, axis=0, keepdims=True
                )


def depth_taps(maps, dz, w_point):
    pixels, channels = maps.shape[1:]
    block = 256
    return pl.pallas_call(
        taps_kernel,
        name="taps",
        grid=(channels // block,),
        out_shape=jax.ShapeDtypeStruct((32, channels), F32),
        in_specs=[
            VMEM,
            VMEM,
            pl.BlockSpec((3, HID, block), lambda j: (0, 0, j)),
        ],
        out_specs=pl.BlockSpec((32, block), lambda j: (0, j)),
        scratch_shapes=[
            pltpu.VMEM((block // LANES, pixels // W16, 2 * PAD + W16, LANES), F32),
            pltpu.VMEM((3, pixels, block), F32),
        ],
        compiler_params=pltpu.CompilerParams(vmem_limit_bytes=16 * 2**20),
        cost_estimate=pl.CostEstimate(
            flops=4_500_000_000, bytes_accessed=4_000_000, transcendentals=0
        ),
    )(maps, dz, w_point)


PRODUCT_COLUMNS = 512


def product_kernel(count, first, *refs):
    out_ref = refs[-1]
    layer, step = first + pl.program_id(0), pl.program_id(1)
    left_columns = pl.ds(pl.multiple_of(layer * HID, HID), HID)
    columns = pl.ds(pl.multiple_of(step * PRODUCT_COLUMNS, PRODUCT_COLUMNS), PRODUCT_COLUMNS)
    total = None
    for left, right in zip(refs[:count], refs[count : 2 * count]):
        right = right[layer, :, columns] if len(right.shape) == 3 else right[:, columns]
        part = dot_tn(left[:, left_columns], right)
        total = part if total is None else total + part
    out_ref[0] = total.astype(BF16)


def products(lefts, rights, first, layers):
    channels = rights[0].shape[-1]
    count = len(lefts)
    return pl.pallas_call(
        functools.partial(product_kernel, count, first),
        name="products",
        grid=(layers, channels // PRODUCT_COLUMNS),
        out_shape=jax.ShapeDtypeStruct((layers, HID, channels), BF16),
        in_specs=[VMEM] * (2 * count),
        out_specs=pl.BlockSpec((1, HID, PRODUCT_COLUMNS), lambda k, j: (k, 0, j)),
        compiler_params=pltpu.CompilerParams(vmem_limit_bytes=10 * 2**20),
        cost_estimate=pl.CostEstimate(
            flops=layers * 2_200_000_000, bytes_accessed=layers * 5_000_000, transcendentals=0
        ),
    )(*lefts, *rights)


STEPS = 4


def update_kernel(
    core_ref,
    rate_ref,
    w_plain,
    w_point,
    w_pool,
    w_proj,
    w_depth,
    b_branch,
    b_proj,
    w_class,
    b_class,
    mine0,
    rest0,
    mine1,
    rest1,
    mine2,
    rest2,
    factors,
    small,
    new_plain,
    new_point,
    new_pool,
    new_proj,
    new_depth,
    new_b_branch,
    new_b_proj,
    new_class,
    new_b_class,
    scale_ref,
    slopes_ref,
    left_ref,
):
    step = pl.program_id(0)
    pairs = ((mine0, rest0), (mine1, rest1), (mine2, rest2))
    count = factors.shape[0]
    arrays = (w_plain, w_point, w_pool, w_proj, w_depth, b_branch, b_proj, w_class, b_class)
    entries = sum(math.prod(array.shape) for array in arrays)

    def outer_squared(a, b):
        product = dot_exact_nt(a, a) * dot_exact_nt(b, b)
        return jnp.sum(product, keepdims=True)

    @pl.when(step == 0)
    def _():
        slopes_ref[...] = jnp.zeros(slopes_ref.shape, F32)
        slopes_ref[:count, :] = factors[:, : 2 * HID]
        left_ref[...] = slopes_ref[...].T
        total = jnp.zeros((16, small.shape[1]), F32)
        for mine, rest in pairs:
            for row in range(0, mine.shape[1], 16):
                for layer in range(mine.shape[0]):
                    one = mine[layer, row : row + 16, :].astype(F32)
                    other = rest[layer, row : row + 16, :].astype(F32)
                    total = total + (one * one + other * other)
        for row in range(0, small.shape[0], 16):
            total = total + jnp.square(small[row : row + 16, :])
        squares = jnp.sum(total, keepdims=True)
        squares = squares + outer_squared(factors[:, :HID], factors[:, 3 * HID :])
        squares = squares + outer_squared(
            factors[:, HID : 2 * HID], factors[:, 2 * HID : 3 * HID]
        )
        norm_scale = jnp.sqrt(squares / entries + 1e-06)
        scale_ref[...] = jnp.broadcast_to(rate_ref[0] / norm_scale, scale_ref.shape)

    scale = scale_ref[0:1, 0:1]

    def large(side):
        rows = new_plain.shape[1]
        here = pl.ds(pl.multiple_of(lax.rem(step, STEPS // 2) * rows, rows), rows)
        there = lax.rem(step + core_ref[0] * (STEPS // 2), STEPS)
        start = pl.multiple_of(there * rows, rows)
        there = pl.ds(start, rows)
        proj, low, high = (
            [pair[side][layer, here, :] for layer in range(pair[side].shape[0])] for pair in pairs
        )
        wide = proj[0].shape[-1]
        new_plain[0] = w_plain[0, there, :] - scale * low[0].astype(F32)
        new_point[0, 0] = w_point[0, 0, there, :] - scale * low[1].astype(F32)
        new_point[0, 1] = w_point[0, 1, there, :] - scale * high[0].astype(F32)
        new_point[0, 2] = w_point[0, 2, there, :] - scale * high[1].astype(F32)
        new_proj[0, :, :wide] = w_proj[0, there, :wide] - scale * proj[0].astype(F32)
        proj4_grad = dot_exact(left_ref[pl.ds(HID + start, rows), :count], factors[:, 2 * HID : 3 * HID])
        new_proj[0, :, wide:] = w_proj[0, there, wide:] - scale * proj4_grad
        pool_grad = dot_exact(left_ref[pl.ds(start, rows), :count], factors[:, 3 * HID :])
        new_pool[0] = w_pool[0, there, :] - scale * pool_grad

    @pl.when(step < STEPS // 2)
    def _():
        large(0)

    @pl.when(step >= STEPS // 2)
    def _():
        large(1)

    @pl.when(step == 0)
    def _():
        for row in range(w_depth.shape[0]):
            new_depth[row] = w_depth[row] - scale * small[row : row + 1, :]
        for branch in range(5):
            row = 32 if branch < 4 else 34
            first = branch % 4 * HID
            new_b_branch[branch] = (
                b_branch[branch] - scale * small[row : row + 1, first : first + HID]
            )
        new_b_proj[...] = b_proj[...] - scale * small[33:34, :HID]
        classes = w_class.shape[0]
        for index in range(classes):
            row, first = 40 + index % 8, index // 8 * HID
            new_class[index] = w_class[index] - scale * small[row : row + 1, first : first + HID]
        new_b_class[...] = b_class[...] - scale * small[35:36, :classes]


def fetch_kernel(*refs):
    count = len(refs) // 3
    copies = [
        pltpu.make_async_copy(source, target, done)
        for source, target, done in zip(refs[:count], refs[count : 2 * count], refs[2 * count :])
    ]
    for copy in copies:
        copy.start()
    for copy in copies:
        copy.wait()


def fetch(arrays):
    return pl.pallas_call(
        fetch_kernel,
        name="fetch",
        out_shape=[pltpu.VMEM(array.shape, array.dtype) for array in arrays],
        in_specs=[pl.BlockSpec(memory_space=pl.ANY)] * len(arrays),
        out_specs=[VMEM] * len(arrays),
        scratch_shapes=[pltpu.SemaphoreType.DMA] * len(arrays),
        compiler_params=pltpu.CompilerParams(vmem_limit_bytes=2**20),
        cost_estimate=pl.CostEstimate(
            flops=3_500_000_000, bytes_accessed=8_000_000, transcendentals=0
        ),
    )(*arrays)


def update(core, rate, params, large, halves, factors, small):
    w_plain, w_depth, w_point, w_pool, b_branch, w_proj, b_proj, w_class, b_class = params
    inputs = tuple(large) + tuple(
        array if array.ndim == 2 else array.reshape(-1, 1, array.shape[-1])
        for array in (w_depth, b_branch, b_proj, w_class, b_class)
    )
    rows, half = HID // STEPS, STEPS // 2

    def where(step, core_ref):
        return lax.rem(step + core_ref[0] * half, STEPS)

    def by_rows(shape):
        if len(shape) == 2:
            return pl.BlockSpec((rows, shape[1]), lambda j, core: (where(j, core), 0))
        if len(shape) == 3:
            return pl.BlockSpec((1, rows, shape[2]), lambda j, core: (0, where(j, core), 0))
        return pl.BlockSpec((1, shape[1], rows, shape[3]), lambda j, core: (0, 0, where(j, core), 0))

    def whole(shape):
        return pl.BlockSpec(shape, lambda j, core: (0,) * len(shape))

    small_specs = [whole(array.shape) for array in inputs[4:]]
    specs = [by_rows(array.shape) for array in inputs[:4]] + small_specs
    new = pl.pallas_call(
        update_kernel,
        name="update",
        out_shape=[jax.ShapeDtypeStruct(array.shape, F32) for array in inputs],
        grid_spec=pltpu.PrefetchScalarGridSpec(
            num_scalar_prefetch=1,
            grid=(STEPS,),
            in_specs=[SMEM]
            + [VMEM] * 4
            + small_specs
            + [VMEM] * (2 * len(halves))
            + [VMEM, VMEM],
            out_specs=specs,
            scratch_shapes=[
                pltpu.VMEM((8, LANES), F32),
                pltpu.VMEM((LANES, 2 * HID), F32),
                pltpu.VMEM((2 * HID, LANES), F32),
            ],
        ),
        compiler_params=pltpu.CompilerParams(vmem_limit_bytes=14 * 2**20),
        cost_estimate=pl.CostEstimate(
            flops=4_000_000, bytes_accessed=20_000_000, transcendentals=0
        ),
    )(core, rate, *inputs, *(array for pair in halves for array in pair), factors, small)
    order = (0, 4, 1, 2, 5, 3, 6, 7, 8)
    return tuple(new[i].reshape(param.shape) for i, param in zip(order, params))


def place(z, y, x):
    return z * 16 + (y % 4) * 4 + x % 4


EVERY = [(z, y, x) for z in range(2) for y in range(4) for x in range(4)]


def along_x(step):
    return [(place(z, y, x), place(z, y, x + step)) for z, y, x in EVERY]


def along_y(step):
    return [(place(z, y, x), place(z, y + step, x)) for z, y, x in EVERY]


ACROSS_Z = [(t, (t + 16) % 32) for t in range(32)]
CORES = [(b, b ^ 1) for b in range(4)]
CHIPS = [(b, b ^ 2) for b in range(4)]


def gather_ring(block, along):
    return (
        block,
        lax.ppermute(block, "trial", along(1)),
        lax.ppermute(block, "trial", along(-1)),
        lax.ppermute(block, "trial", along(2)),
    )


def from_batch(mine):
    return [mine] + [
        lax.ppermute(mine, "batch", [(b, b ^ other) for b in range(4)]) for other in (1, 2, 3)
    ]


def in_order(parts, core, chip):
    near, beside, across, beyond = parts
    low = jnp.where(core == 0, jnp.concatenate([near, beside]), jnp.concatenate([beside, near]))
    high = jnp.where(core == 0, jnp.concatenate([across, beyond]), jnp.concatenate([beyond, across]))
    return jnp.where(chip == 0, jnp.concatenate([low, high]), jnp.concatenate([high, low]))


def sum_cores(partial, core):
    half = partial.shape[1] // 2
    mine = lax.dynamic_slice_in_dim(partial, core * half, half, 1)
    other = lax.dynamic_slice_in_dim(partial, (1 - core) * half, half, 1)
    return (mine.astype(F32) + lax.ppermute(other, "batch", CORES).astype(F32)).astype(BF16)


def sum_chips(pair):
    return (pair.astype(F32) + lax.ppermute(pair, "batch", CHIPS).astype(F32)).astype(BF16)


def sum_batch_small(partial):
    near, beside, across, beyond = [part.astype(F32) for part in from_batch(partial)]
    return (near + beside) + (across + beyond)


def pick(table, plan, turn_ids):
    return jnp.stack(
        [lax.dynamic_index_in_dim(table, plan[m], 0, keepdims=False) for m in turn_ids]
    )


def pool_map(coarse):
    return (jnp.sum(coarse, axis=-1, dtype=F32) / coarse.shape[-1]).astype(BF16)


def on_device(
    features16,
    features32,
    labels,
    plan,
    lr_index,
    w_plain,
    w_depth,
    w_point,
    w_pool,
    b_branch,
    w_proj,
    b_proj,
    w_class,
    b_class,
):
    turns = plan.shape[0]
    trial = lax.axis_index("trial")
    batch = lax.axis_index("batch")
    core, chip = batch % 2, batch // 2
    where = jnp.stack([trial % 4, (trial // 4) % 4, trial // 16]).astype(jnp.int32)

    own = features16[0, 0].T
    channels = own.shape[1]
    pieces = lax.all_to_all(own.reshape(32, 16, channels), "trial", 0, 0, tiled=True)
    turn_lists = [list(range(order, turns, 2)) for order in range(2)]
    picked = pick(pieces, plan, turn_lists[0] + turn_lists[1])
    pooled = pool_map(features32[0, 0]).reshape(-1, 1, channels)
    pooled = jnp.where((plan == trial)[None, :, None], pooled, jnp.zeros((), BF16))
    pooled = pooled.reshape(-1, channels)
    rows = pooled.shape[0]
    across = lax.ppermute(
        jnp.concatenate([picked.reshape(-1, channels), pooled]), "trial", ACROSS_Z
    )
    pooled = pooled + across[-rows:]
    across = across[:-rows].reshape(picked.shape)
    blocks, outers = [None] * turns, [None] * turns
    for order, (inner, outer) in enumerate(((along_y, along_x), (along_x, along_y))):
        turn_ids = turn_lists[order]
        count = len(turn_ids)
        some = slice(order * len(turn_lists[0]), order * len(turn_lists[0]) + count)
        block = jnp.stack([picked[some], across[some]], axis=1).reshape(-1, channels)
        size = block.shape[0]
        if order == 0:
            block = jnp.concatenate([block, pooled])
        ring = gather_ring(block, inner)
        if order == 0:
            pooled = sum(part[size:] for part in ring)
        for place_in, m in enumerate(turn_ids):
            first, last = place_in * size // count, (place_in + 1) * size // count
            parts = [part[first:last] for part in ring]
            blocks[m] = jnp.concatenate(parts + [pooled] if m == 0 else parts)
            outers[m] = outer
    after = lax.optimization_barrier
    maps = [gather_ring(blocks[m], outers[m]) for m in range(2)]
    pooled = sum(part[4 * size // count :] for part in maps[0])
    pooled = [pooled[first : first + turns] for first in range(0, rows, turns)]

    point16 = w_point[0].astype(BF16)
    proj16 = w_proj[0].astype(BF16)
    taps = w_depth.reshape(27, 1, -1)
    classes = w_class.shape[1]
    class16 = jnp.pad(w_class[0].astype(BF16), ((0, 32 - classes), (0, 0)))
    class_bias = jnp.pad(b_class[0], (0, 32 - classes), constant_values=-1e30)[:, None]
    wide = 4 * HID
    pool16 = w_pool[0].astype(BF16)
    branch4 = sum(
        dot_nt(part, pool16[:, i * channels : (i + 1) * channels]) for i, part in enumerate(pooled)
    )
    branch4 = jax.nn.relu(branch4 + b_branch[0, 4]).astype(BF16)
    proj_bias = dot_nt(branch4, proj16[:, wide:]) + b_proj[0]
    marks = pick(labels[:, 0], plan, range(turns))

    fronts = []
    for m in range(turns):
        if m >= 2:
            maps.append(gather_ring(blocks[m], outers[m]))
        weights = (
            w_plain[0].astype(BF16),
            taps,
            point16,
            b_branch[0, :4].reshape(1, wide),
            proj16[:, :wide],
            proj_bias[m : m + 1],
            class16,
            class_bias,
        )
        if m == 0:
            maps[0], blocks[2] = after((maps[0], blocks[2]))
        fronts.append(front(m % 2, where, maps[m], marks[m : m + 1], weights))
        if m == 0:
            fronts[0], maps[1], blocks[3] = after((fronts[0], maps[1], blocks[3]))
    stacks, joined, dpres, dzs, sums, dclass = zip(*fronts)

    dbias_proj = jnp.stack([part[1, :HID] for part in sums])
    dbranch4 = dot_exact(dbias_proj, proj16[:, wide:].astype(F32))
    dbranch4 = jnp.where(branch4 > 0, dbranch4, 0.0)
    factors = [dbranch4, dbias_proj, branch4] + pooled
    factors = jnp.concatenate([part.astype(F32) for part in factors], axis=1)
    factors = from_batch(jnp.pad(factors, ((0, 8 - turns), (0, 0))))
    proj_part = products(dpres, joined, 0, 1)
    dzs, proj_part = after((dzs, proj_part))
    proj_pair = sum_cores(proj_part, core)
    low_part = products(dzs, stacks, 0, 2)
    dzs, low_part, proj_pair = after((dzs, low_part, proj_pair))
    low_pair = sum_cores(low_part, core)
    high_part = products(dzs, stacks, 2, 2)
    proj_total = sum_chips(proj_pair)
    dzs, high_part, low_pair, factors = after((dzs, high_part, low_pair, factors))
    high_pair = sum_cores(high_part, core)
    low_total = sum_chips(low_pair)
    taps_parts = [depth_taps(stacks[0], dzs[0], point16)]
    dzs, taps_parts, high_pair = after((dzs, taps_parts, high_pair))
    taps_parts.append(depth_taps(stacks[1], dzs[1], point16))
    dzs, taps_parts, proj_total = after((dzs, taps_parts, proj_total))
    proj_rest = lax.ppermute(proj_total, "batch", CORES)
    taps_parts.append(depth_taps(stacks[2], dzs[2], point16))
    dzs, taps_parts, proj_rest = after((dzs, taps_parts, proj_rest))
    taps_parts.append(depth_taps(stacks[3], dzs[3], point16))
    depth_part = sum(taps_parts)
    factors, depth_part = after((factors, depth_part))
    factors = in_order(factors, core, chip)
    dclass = sum(dclass)
    bias_row = jnp.pad(jnp.sum(dbranch4, axis=0)[None], ((2, 5), (0, wide - HID)))
    small = jnp.concatenate(
        [
            depth_part,
            sum(sums) + bias_row,
            jnp.concatenate([dclass[8 * g : 8 * g + 8] for g in range(4)], axis=1),
        ]
    )
    small = sum_batch_small(small.astype(BF16))
    high_other = lax.ppermute(high_pair, "batch", CHIPS)
    large, factors = after(((w_plain, w_point, w_pool, w_proj), factors))
    high_other, low_total, large, small = after((high_other, low_total, fetch(large), small))
    high_total = (high_pair.astype(F32) + high_other.astype(F32)).astype(BF16)
    halves = [(proj_total, proj_rest)]
    halves += [(total, lax.ppermute(total, "batch", CORES)) for total in (low_total, high_total)]

    params = (w_plain, w_depth, w_point, w_pool, b_branch, w_proj, b_proj, w_class, b_class)

    step_rate = 0.5 * jnp.exp2(-6.0 * lr_index[0].astype(F32) / 1073741824.0)
    return update(
        core.reshape(1).astype(jnp.int32), step_rate.reshape(1), params, large, halves, factors, small
    )


def solution(mesh):
    in_specs = (
        P("trial", "batch", None, None),
        P("trial", "batch", None, None),
        P(None, "batch", None),
        P(),
        P("trial"),
        P("trial", None, None),
        P("trial", None, None, None),
        P("trial", None, None, None),
        P("trial", None, None),
        P("trial", None, None),
        P("trial", None, None),
        P("trial", None),
        P("trial", None, None),
        P("trial", None),
    )
    out_specs = (
        P("trial", None, None),
        P("trial", None, None, None),
        P("trial", None, None, None),
        P("trial", None, None),
        P("trial", None, None),
        P("trial", None, None),
        P("trial", None),
        P("trial", None, None),
        P("trial", None),
    )
    return jax.shard_map(
        on_device, mesh=mesh, in_specs=in_specs, out_specs=out_specs, check_vma=False
    )
```

```python
import functools
import math

import jax
import jax.numpy as jnp
from jax import lax
from jax.experimental import pallas as pl
from jax.experimental.pallas import tpu as pltpu
from jax.sharding import PartitionSpec as P

W16 = 32
HID = 256
PAD = 24
DILATIONS = (6, 12, 18)
LANES = 128
RELATIVE = (0, -1, 1, 2)
BF16 = jnp.bfloat16
F32 = jnp.float32


def dot_nt(a, b):
    return lax.dot_general(a, b, (((1,), (1,)), ((), ())), preferred_element_type=F32)


def dot_nn(a, b):
    return lax.dot_general(a, b, (((1,), (0,)), ((), ())), preferred_element_type=F32)


def dot_exact(a, b):
    return lax.dot_general(
        a,
        b,
        (((1,), (0,)), ((), ())),
        precision=lax.Precision.HIGHEST,
        preferred_element_type=F32,
    )


def dot_exact_nt(a, b):
    return lax.dot_general(
        a,
        b,
        (((1,), (1,)), ((), ())),
        precision=lax.Precision.HIGHEST,
        preferred_element_type=F32,
    )


def dot_tn(a, b):
    return lax.dot_general(a, b, (((0,), (0,)), ((), ())), preferred_element_type=F32)


def taps_of_row(row, rows, dilation):
    taps = []
    for a in (-1, 0, 1):
        source = row + a * dilation
        if 0 <= source < rows:
            for b in (-1, 0, 1):
                taps.append((3 * (a + 1) + (b + 1), source, b * dilation))
    return taps


def clear_margins(padded):
    rows = padded.shape[0]
    blank = jnp.zeros((rows, PAD, LANES), F32)
    padded[:, 0:PAD, :] = blank
    padded[:, PAD + W16 : 2 * PAD + W16, :] = blank


def fill_padded(padded, x_ref, lanes):
    for row in range(padded.shape[0]):
        padded[row, PAD : PAD + W16, :] = x_ref[row * W16 : (row + 1) * W16, lanes].astype(F32)


def front_kernel(
    order,
    where_ref,
    piece0,
    piece1,
    piece2,
    piece3,
    marks,
    w_plain,
    w_depth,
    w_point,
    bias,
    w_proj,
    proj_bias,
    w_class,
    class_bias,
    maps_ref,
    joined_ref,
    dpre_ref,
    dz_ref,
    sums_ref,
    dclass_ref,
    padded,
):
    x_ref = maps_ref.at[0]
    x, y, z = where_ref[0], where_ref[1], where_ref[2]
    for outer, piece in enumerate((piece0, piece1, piece2, piece3)):
        for inner in range(4):
            far, near = RELATIVE[outer] + 4, RELATIVE[inner] + 4
            if order == 0:
                xx, yy = lax.rem(x + far, 4), lax.rem(y + near, 4)
            else:
                xx, yy = lax.rem(x + near, 4), lax.rem(y + far, 4)
            for k in range(2):
                zz = z if k == 0 else 1 - z
                start = pl.multiple_of((zz * 16 + yy * 4 + xx) * 16, 16)
                x_ref[pl.ds(start, 16), :] = piece[pl.ds((2 * inner + k) * 16, 16), :]
    rows = padded.shape[0]
    clear_margins(padded)

    def chunk(j, carry):
        lanes = pl.ds(pl.multiple_of(j * LANES, LANES), LANES)
        fill_padded(padded, x_ref, lanes)
        for k, dilation in enumerate(DILATIONS):
            for row in range(rows):
                total = jnp.zeros((W16, LANES), F32)
                for tap, source, shift in taps_of_row(row, rows, dilation):
                    weight = w_depth[9 * k + tap, :, lanes]
                    total = total + weight * padded[source, PAD + shift : PAD + shift + W16, :]
                maps_ref[k + 1, row * W16 : (row + 1) * W16, lanes] = total.astype(BF16)
        return carry

    lax.fori_loop(0, x_ref.shape[1] // LANES, chunk, 0)

    for branch in range(4):
        columns = slice(branch * HID, (branch + 1) * HID)
        if branch == 0:
            pre = dot_nt(x_ref[...], w_plain[...])
        else:
            pre = dot_nt(maps_ref[branch], w_point[branch - 1])
        joined_ref[:, columns] = jnp.maximum(pre + bias[:, columns], 0.0).astype(BF16)
    hidden = jnp.maximum(dot_nt(joined_ref[...], w_proj[...]) + proj_bias[...], 0.0).astype(BF16)
    logits = dot_nt(w_class[...], hidden) + class_bias[...]
    top = jnp.max(logits, axis=0, keepdims=True)
    raised = jnp.exp(logits - top)
    share = raised / jnp.sum(raised, axis=0, keepdims=True)
    class_ids = lax.broadcasted_iota(jnp.int32, logits.shape, 0)
    dlogits = share - jnp.where(class_ids == marks[...], 1.0, 0.0)
    square = (logits.shape[0], LANES)
    column = jnp.broadcast_to(jnp.sum(dlogits, axis=1, keepdims=True), square)
    on_diagonal = lax.broadcasted_iota(jnp.int32, square, 0) == lax.broadcasted_iota(
        jnp.int32, square, 1
    )
    short = dlogits.astype(BF16)
    dclass_ref[...] = dot_nn(short, hidden)
    dhidden = dot_tn(short, w_class[...])
    dpre = jnp.where(hidden.astype(F32) > 0, dhidden, 0.0)
    dpre_short = dpre.astype(BF16)
    dpre_ref[...] = dpre_short
    sums_ref[...] = jnp.zeros(sums_ref.shape, F32)
    sums_ref[3:4, 0:LANES] = jnp.sum(jnp.where(on_diagonal, column, 0.0), axis=0, keepdims=True)
    sums_ref[1:2, 0:HID] = jnp.sum(dpre_short.astype(F32), axis=0, keepdims=True)
    for branch in range(4):
        columns = slice(branch * HID, (branch + 1) * HID)
        djoined = dot_nn(dpre_short, w_proj[:, columns])
        dz = jnp.where(joined_ref[:, columns].astype(F32) > 0, djoined, 0.0).astype(BF16)
        dz_ref[:, columns] = dz
        sums_ref[0:1, columns] = jnp.sum(dz.astype(F32), axis=0, keepdims=True)


VMEM = pl.BlockSpec(memory_space=pltpu.VMEM)
SMEM = pl.BlockSpec(memory_space=pltpu.SMEM)


def front(order, where, pieces, marks, weights):
    pixels, channels = marks.shape[1], weights[0].shape[1]
    shapes = (
        ((4, pixels, channels), BF16),
        ((pixels, 4 * HID), BF16),
        ((pixels, HID), BF16),
        ((pixels, 4 * HID), BF16),
        ((8, 4 * HID), F32),
        ((32, HID), F32),
    )
    return pl.pallas_call(
        functools.partial(front_kernel, order),
        name="front",
        out_shape=[pltpu.VMEM(*shape) for shape in shapes],
        in_specs=[SMEM] + [VMEM] * (4 + 1 + len(weights)),
        out_specs=[VMEM] * len(shapes),
        scratch_shapes=[pltpu.VMEM((pixels // W16, 2 * PAD + W16, LANES), F32)],
        compiler_params=pltpu.CompilerParams(vmem_limit_bytes=16 * 2**20),
        cost_estimate=pl.CostEstimate(
            flops=6_700_000_000, bytes_accessed=12_000_000, transcendentals=16384
        ),
    )(where, *pieces, marks, *weights)


def taps_kernel(maps_ref, dz_ref, w_point, out_ref, padded, ddepth):
    x_ref = maps_ref.at[0]
    rows = padded.shape[1]
    halves = padded.shape[0]
    for half in range(halves):
        start = pl.multiple_of((pl.program_id(0) * halves + half) * LANES, LANES)
        clear_margins(padded.at[half])
        fill_padded(padded.at[half], x_ref, pl.ds(start, LANES))
    out_ref[...] = jnp.zeros(out_ref.shape, F32)
    for k, dilation in enumerate(DILATIONS):
        back = dot_nn(dz_ref[:, (k + 1) * HID : (k + 2) * HID], w_point[k])
        ddepth[k] = back.astype(BF16).astype(F32)
    for half in range(halves):
        lanes = slice(half * LANES, (half + 1) * LANES)
        for k, dilation in enumerate(DILATIONS):
            totals = {}
            for row in range(rows):
                slope = ddepth[k, row * W16 : (row + 1) * W16, lanes]
                for tap, source, shift in taps_of_row(row, rows, dilation):
                    value = slope * padded[half, source, PAD + shift : PAD + shift + W16, :]
                    value = jnp.sum(value.reshape(W16 // 8, 8, LANES), axis=0)
                    totals[tap] = value if tap not in totals else totals[tap] + value
            for tap, value in totals.items():
                out_ref[9 * k + tap : 9 * k + tap + 1, lanes] = jnp.sum(
                    value, axis=0, keepdims=True
                )


def depth_taps(maps, dz, w_point):
    pixels, channels = maps.shape[1:]
    block = 256
    return pl.pallas_call(
        taps_kernel,
        name="taps",
        grid=(channels // block,),
        out_shape=jax.ShapeDtypeStruct((32, channels), F32),
        in_specs=[
            VMEM,
            VMEM,
            pl.BlockSpec((3, HID, block), lambda j: (0, 0, j)),
        ],
        out_specs=pl.BlockSpec((32, block), lambda j: (0, j)),
        scratch_shapes=[
            pltpu.VMEM((block // LANES, pixels // W16, 2 * PAD + W16, LANES), F32),
            pltpu.VMEM((3, pixels, block), F32),
        ],
        compiler_params=pltpu.CompilerParams(vmem_limit_bytes=16 * 2**20),
        cost_estimate=pl.CostEstimate(
            flops=4_500_000_000, bytes_accessed=4_000_000, transcendentals=0
        ),
    )(maps, dz, w_point)


PRODUCT_COLUMNS = 512


def product_kernel(count, first, *refs):
    out_ref = refs[-1]
    layer, step = first + pl.program_id(0), pl.program_id(1)
    left_columns = pl.ds(pl.multiple_of(layer * HID, HID), HID)
    columns = pl.ds(pl.multiple_of(step * PRODUCT_COLUMNS, PRODUCT_COLUMNS), PRODUCT_COLUMNS)
    total = None
    for left, right in zip(refs[:count], refs[count : 2 * count]):
        right = right[layer, :, columns] if len(right.shape) == 3 else right[:, columns]
        part = dot_tn(left[:, left_columns], right)
        total = part if total is None else total + part
    out_ref[0] = total.astype(BF16)


def products(lefts, rights, first, layers):
    channels = rights[0].shape[-1]
    count = len(lefts)
    return pl.pallas_call(
        functools.partial(product_kernel, count, first),
        name="products",
        grid=(layers, channels // PRODUCT_COLUMNS),
        out_shape=jax.ShapeDtypeStruct((layers, HID, channels), BF16),
        in_specs=[VMEM] * (2 * count),
        out_specs=pl.BlockSpec((1, HID, PRODUCT_COLUMNS), lambda k, j: (k, 0, j)),
        compiler_params=pltpu.CompilerParams(vmem_limit_bytes=10 * 2**20),
        cost_estimate=pl.CostEstimate(
            flops=layers * 2_200_000_000, bytes_accessed=layers * 5_000_000, transcendentals=0
        ),
    )(*lefts, *rights)


STEPS = 4


def update_kernel(
    core_ref,
    rate_ref,
    w_plain,
    w_point,
    w_pool,
    w_proj,
    w_depth,
    b_branch,
    b_proj,
    w_class,
    b_class,
    mine0,
    rest0,
    mine1,
    rest1,
    mine2,
    rest2,
    factors,
    small,
    new_plain,
    new_point,
    new_pool,
    new_proj,
    new_depth,
    new_b_branch,
    new_b_proj,
    new_class,
    new_b_class,
    scale_ref,
    slopes_ref,
    left_ref,
):
    step = pl.program_id(0)
    pairs = ((mine0, rest0), (mine1, rest1), (mine2, rest2))
    count = factors.shape[0]
    arrays = (w_plain, w_point, w_pool, w_proj, w_depth, b_branch, b_proj, w_class, b_class)
    entries = sum(math.prod(array.shape) for array in arrays)

    def outer_squared(a, b):
        product = dot_exact_nt(a, a) * dot_exact_nt(b, b)
        return jnp.sum(product, keepdims=True)

    @pl.when(step == 0)
    def _():
        slopes_ref[...] = jnp.zeros(slopes_ref.shape, F32)
        slopes_ref[:count, :] = factors[:, : 2 * HID]
        left_ref[...] = slopes_ref[...].T
        total = jnp.zeros((16, small.shape[1]), F32)
        for mine, rest in pairs:
            for row in range(0, mine.shape[1], 16):
                for layer in range(mine.shape[0]):
                    one = mine[layer, row : row + 16, :].astype(F32)
                    other = rest[layer, row : row + 16, :].astype(F32)
                    total = total + (one * one + other * other)
        for row in range(0, small.shape[0], 16):
            total = total + jnp.square(small[row : row + 16, :])
        squares = jnp.sum(total, keepdims=True)
        squares = squares + outer_squared(factors[:, :HID], factors[:, 3 * HID :])
        squares = squares + outer_squared(
            factors[:, HID : 2 * HID], factors[:, 2 * HID : 3 * HID]
        )
        norm_scale = jnp.sqrt(squares / entries + 1e-06)
        scale_ref[...] = jnp.broadcast_to(rate_ref[0] / norm_scale, scale_ref.shape)

    scale = scale_ref[0:1, 0:1]

    def large(side):
        rows = new_plain.shape[1]
        here = pl.ds(pl.multiple_of(lax.rem(step, STEPS // 2) * rows, rows), rows)
        there = lax.rem(step + core_ref[0] * (STEPS // 2), STEPS)
        start = pl.multiple_of(there * rows, rows)
        there = pl.ds(start, rows)
        proj, low, high = (
            [pair[side][layer, here, :] for layer in range(pair[side].shape[0])] for pair in pairs
        )
        wide = proj[0].shape[-1]
        new_plain[0] = w_plain[0, there, :] - scale * low[0].astype(F32)
        new_point[0, 0] = w_point[0, 0, there, :] - scale * low[1].astype(F32)
        new_point[0, 1] = w_point[0, 1, there, :] - scale * high[0].astype(F32)
        new_point[0, 2] = w_point[0, 2, there, :] - scale * high[1].astype(F32)
        new_proj[0, :, :wide] = w_proj[0, there, :wide] - scale * proj[0].astype(F32)
        proj4_grad = dot_exact(left_ref[pl.ds(HID + start, rows), :count], factors[:, 2 * HID : 3 * HID])
        new_proj[0, :, wide:] = w_proj[0, there, wide:] - scale * proj4_grad
        pool_grad = dot_exact(left_ref[pl.ds(start, rows), :count], factors[:, 3 * HID :])
        new_pool[0] = w_pool[0, there, :] - scale * pool_grad

    @pl.when(step < STEPS // 2)
    def _():
        large(0)

    @pl.when(step >= STEPS // 2)
    def _():
        large(1)

    @pl.when(step == 0)
    def _():
        for row in range(w_depth.shape[0]):
            new_depth[row] = w_depth[row] - scale * small[row : row + 1, :]
        for branch in range(5):
            row = 32 if branch < 4 else 34
            first = branch % 4 * HID
            new_b_branch[branch] = (
                b_branch[branch] - scale * small[row : row + 1, first : first + HID]
            )
        new_b_proj[...] = b_proj[...] - scale * small[33:34, :HID]
        classes = w_class.shape[0]
        for index in range(classes):
            row, first = 40 + index % 8, index // 8 * HID
            new_class[index] = w_class[index] - scale * small[row : row + 1, first : first + HID]
        new_b_class[...] = b_class[...] - scale * small[35:36, :classes]


def fetch_kernel(*refs):
    count = len(refs) // 3
    copies = [
        pltpu.make_async_copy(source, target, done)
        for source, target, done in zip(refs[:count], refs[count : 2 * count], refs[2 * count :])
    ]
    for copy in copies:
        copy.start()
    for copy in copies:
        copy.wait()


def fetch(arrays):
    return pl.pallas_call(
        fetch_kernel,
        name="fetch",
        out_shape=[pltpu.VMEM(array.shape, array.dtype) for array in arrays],
        in_specs=[pl.BlockSpec(memory_space=pl.ANY)] * len(arrays),
        out_specs=[VMEM] * len(arrays),
        scratch_shapes=[pltpu.SemaphoreType.DMA] * len(arrays),
        compiler_params=pltpu.CompilerParams(vmem_limit_bytes=2**20),
        cost_estimate=pl.CostEstimate(
            flops=3_500_000_000, bytes_accessed=8_000_000, transcendentals=0
        ),
    )(*arrays)


def update(core, rate, params, large, halves, factors, small):
    w_plain, w_depth, w_point, w_pool, b_branch, w_proj, b_proj, w_class, b_class = params
    inputs = tuple(large) + tuple(
        array if array.ndim == 2 else array.reshape(-1, 1, array.shape[-1])
        for array in (w_depth, b_branch, b_proj, w_class, b_class)
    )
    rows, half = HID // STEPS, STEPS // 2

    def where(step, core_ref):
        return lax.rem(step + core_ref[0] * half, STEPS)

    def by_rows(shape):
        if len(shape) == 2:
            return pl.BlockSpec((rows, shape[1]), lambda j, core: (where(j, core), 0))
        if len(shape) == 3:
            return pl.BlockSpec((1, rows, shape[2]), lambda j, core: (0, where(j, core), 0))
        return pl.BlockSpec((1, shape[1], rows, shape[3]), lambda j, core: (0, 0, where(j, core), 0))

    def whole(shape):
        return pl.BlockSpec(shape, lambda j, core: (0,) * len(shape))

    small_specs = [whole(array.shape) for array in inputs[4:]]
    specs = [by_rows(array.shape) for array in inputs[:4]] + small_specs
    new = pl.pallas_call(
        update_kernel,
        name="update",
        out_shape=[jax.ShapeDtypeStruct(array.shape, F32) for array in inputs],
        grid_spec=pltpu.PrefetchScalarGridSpec(
            num_scalar_prefetch=1,
            grid=(STEPS,),
            in_specs=[SMEM]
            + [VMEM] * 4
            + small_specs
            + [VMEM] * (2 * len(halves))
            + [VMEM, VMEM],
            out_specs=specs,
            scratch_shapes=[
                pltpu.VMEM((8, LANES), F32),
                pltpu.VMEM((LANES, 2 * HID), F32),
                pltpu.VMEM((2 * HID, LANES), F32),
            ],
        ),
        compiler_params=pltpu.CompilerParams(vmem_limit_bytes=14 * 2**20),
        cost_estimate=pl.CostEstimate(
            flops=4_000_000, bytes_accessed=20_000_000, transcendentals=0
        ),
    )(core, rate, *inputs, *(array for pair in halves for array in pair), factors, small)
    order = (0, 4, 1, 2, 5, 3, 6, 7, 8)
    return tuple(new[i].reshape(param.shape) for i, param in zip(order, params))


def place(z, y, x):
    return z * 16 + (y % 4) * 4 + x % 4


EVERY = [(z, y, x) for z in range(2) for y in range(4) for x in range(4)]


def along_x(step):
    return [(place(z, y, x), place(z, y, x + step)) for z, y, x in EVERY]


def along_y(step):
    return [(place(z, y, x), place(z, y + step, x)) for z, y, x in EVERY]


ACROSS_Z = [(t, (t + 16) % 32) for t in range(32)]
CORES = [(b, b ^ 1) for b in range(4)]
CHIPS = [(b, b ^ 2) for b in range(4)]


def gather_ring(block, along):
    return (
        block,
        lax.ppermute(block, "trial", along(1)),
        lax.ppermute(block, "trial", along(-1)),
        lax.ppermute(block, "trial", along(2)),
    )


def from_batch(mine):
    return [mine] + [
        lax.ppermute(mine, "batch", [(b, b ^ other) for b in range(4)]) for other in (1, 2, 3)
    ]


def in_order(parts, core, chip):
    near, beside, across, beyond = parts
    low = jnp.where(core == 0, jnp.concatenate([near, beside]), jnp.concatenate([beside, near]))
    high = jnp.where(core == 0, jnp.concatenate([across, beyond]), jnp.concatenate([beyond, across]))
    return jnp.where(chip == 0, jnp.concatenate([low, high]), jnp.concatenate([high, low]))


def sum_cores(partial, core):
    half = partial.shape[1] // 2
    mine = lax.dynamic_slice_in_dim(partial, core * half, half, 1)
    other = lax.dynamic_slice_in_dim(partial, (1 - core) * half, half, 1)
    return (mine.astype(F32) + lax.ppermute(other, "batch", CORES).astype(F32)).astype(BF16)


def sum_chips(pair):
    return (pair.astype(F32) + lax.ppermute(pair, "batch", CHIPS).astype(F32)).astype(BF16)


def sum_batch_small(partial):
    pair = partial.astype(F32) + lax.ppermute(partial, "batch", CORES).astype(F32)
    pair = pair.astype(BF16)
    return pair.astype(F32) + lax.ppermute(pair, "batch", CHIPS).astype(F32)


def pick(table, plan, turn_ids):
    return jnp.stack(
        [lax.dynamic_index_in_dim(table, plan[m], 0, keepdims=False) for m in turn_ids]
    )


def pool_map(coarse):
    return (jnp.sum(coarse, axis=-1, dtype=F32) / coarse.shape[-1]).astype(BF16)


def on_device(
    features16,
    features32,
    labels,
    plan,
    lr_index,
    w_plain,
    w_depth,
    w_point,
    w_pool,
    b_branch,
    w_proj,
    b_proj,
    w_class,
    b_class,
):
    turns = plan.shape[0]
    trial = lax.axis_index("trial")
    batch = lax.axis_index("batch")
    core, chip = batch % 2, batch // 2
    where = jnp.stack([trial % 4, (trial // 4) % 4, trial // 16]).astype(jnp.int32)

    own = features16[0, 0].T
    channels = own.shape[1]
    pieces = lax.all_to_all(own.reshape(32, 16, channels), "trial", 0, 0, tiled=True)
    turn_lists = [list(range(order, turns, 2)) for order in range(2)]
    picked = pick(pieces, plan, turn_lists[0] + turn_lists[1])
    pooled = pool_map(features32[0, 0]).reshape(-1, 1, channels)
    pooled = jnp.where((plan == trial)[None, :, None], pooled, jnp.zeros((), BF16))
    pooled = pooled.reshape(-1, channels)
    rows = pooled.shape[0]
    across = lax.ppermute(
        jnp.concatenate([picked.reshape(-1, channels), pooled]), "trial", ACROSS_Z
    )
    pooled = pooled + across[-rows:]
    across = across[:-rows].reshape(picked.shape)
    blocks, outers = [None] * turns, [None] * turns
    for order, (inner, outer) in enumerate(((along_y, along_x), (along_x, along_y))):
        turn_ids = turn_lists[order]
        count = len(turn_ids)
        some = slice(order * len(turn_lists[0]), order * len(turn_lists[0]) + count)
        block = jnp.stack([picked[some], across[some]], axis=1).reshape(-1, channels)
        size = block.shape[0]
        if order == 0:
            block = jnp.concatenate([block, pooled])
        ring = gather_ring(block, inner)
        if order == 0:
            pooled = sum(part[size:] for part in ring)
        for place_in, m in enumerate(turn_ids):
            first, last = place_in * size // count, (place_in + 1) * size // count
            parts = [part[first:last] for part in ring]
            blocks[m] = jnp.concatenate(parts + [pooled] if m == 0 else parts)
            outers[m] = outer
    after = lax.optimization_barrier
    maps = [gather_ring(blocks[m], outers[m]) for m in range(2)]
    pooled = sum(part[4 * size // count :] for part in maps[0])
    pooled = [pooled[first : first + turns] for first in range(0, rows, turns)]

    point16 = w_point[0].astype(BF16)
    proj16 = w_proj[0].astype(BF16)
    taps = w_depth.reshape(27, 1, -1)
    classes = w_class.shape[1]
    class16 = jnp.pad(w_class[0].astype(BF16), ((0, 32 - classes), (0, 0)))
    class_bias = jnp.pad(b_class[0], (0, 32 - classes), constant_values=-1e30)[:, None]
    wide = 4 * HID
    pool16 = w_pool[0].astype(BF16)
    branch4 = sum(
        dot_nt(part, pool16[:, i * channels : (i + 1) * channels]) for i, part in enumerate(pooled)
    )
    branch4 = jax.nn.relu(branch4 + b_branch[0, 4]).astype(BF16)
    proj_bias = dot_nt(branch4, proj16[:, wide:]) + b_proj[0]
    marks = pick(labels[:, 0], plan, range(turns))

    fronts = []
    for m in range(turns):
        if m >= 2:
            maps.append(gather_ring(blocks[m], outers[m]))
        weights = (
            w_plain[0].astype(BF16),
            taps,
            point16,
            b_branch[0, :4].reshape(1, wide),
            proj16[:, :wide],
            proj_bias[m : m + 1],
            class16,
            class_bias,
        )
        if m == 0:
            maps[0], blocks[2] = after((maps[0], blocks[2]))
        fronts.append(front(m % 2, where, maps[m], marks[m : m + 1], weights))
        if m == 0:
            fronts[0], maps[1], blocks[3] = after((fronts[0], maps[1], blocks[3]))
    stacks, joined, dpres, dzs, sums, dclass = zip(*fronts)

    dbias_proj = jnp.stack([part[1, :HID] for part in sums])
    dbranch4 = dot_exact(dbias_proj, proj16[:, wide:].astype(F32))
    dbranch4 = jnp.where(branch4 > 0, dbranch4, 0.0)
    factors = [dbranch4, dbias_proj, branch4] + pooled
    factors = jnp.concatenate([part.astype(F32) for part in factors], axis=1)
    factors = from_batch(factors)
    proj_part = products(dpres, joined, 0, 1)
    proj_pair = sum_cores(proj_part, core)
    dzs, proj_pair = after((dzs, proj_pair))
    low_part = products(dzs, stacks, 0, 2)
    proj_total = sum_chips(proj_pair)
    dzs, low_part, proj_total = after((dzs, low_part, proj_total))
    low_pair = sum_cores(low_part, core)
    high_part = products(dzs, stacks, 2, 2)
    dzs, high_part, low_pair, factors = after((dzs, high_part, low_pair, factors))
    high_pair = sum_cores(high_part, core)
    low_total = sum_chips(low_pair)
    taps_parts = [depth_taps(stacks[0], dzs[0], point16)]
    dzs, taps_parts, high_pair = after((dzs, taps_parts, high_pair))
    taps_parts.append(depth_taps(stacks[1], dzs[1], point16))
    dzs, taps_parts, proj_total = after((dzs, taps_parts, proj_total))
    proj_rest = lax.ppermute(proj_total, "batch", CORES)
    taps_parts.append(depth_taps(stacks[2], dzs[2], point16))
    dzs, taps_parts, proj_rest = after((dzs, taps_parts, proj_rest))
    taps_parts.append(depth_taps(stacks[3], dzs[3], point16))
    depth_part = sum(taps_parts)
    factors, depth_part = after((factors, depth_part))
    factors = [jnp.pad(part, ((0, 8 - turns), (0, 0))) for part in factors]
    factors = in_order(factors, core, chip)
    dclass = sum(dclass)
    bias_row = jnp.pad(jnp.sum(dbranch4, axis=0)[None], ((2, 5), (0, wide - HID)))
    small = jnp.concatenate(
        [
            depth_part,
            sum(sums) + bias_row,
            jnp.concatenate([dclass[8 * g : 8 * g + 8] for g in range(4)], axis=1),
        ]
    )
    small = sum_batch_small(small.astype(BF16))
    high_other = lax.ppermute(high_pair, "batch", CHIPS)
    large, factors = after(((w_plain, w_point, w_pool, w_proj), factors))
    high_other, low_total, large, small = after((high_other, low_total, fetch(large), small))
    high_total = (high_pair.astype(F32) + high_other.astype(F32)).astype(BF16)
    halves = [(proj_total, proj_rest)]
    halves += [(total, lax.ppermute(total, "batch", CORES)) for total in (low_total, high_total)]

    params = (w_plain, w_depth, w_point, w_pool, b_branch, w_proj, b_proj, w_class, b_class)

    step_rate = 0.5 * jnp.exp2(-6.0 * lr_index[0].astype(F32) / 1073741824.0)
    return update(
        core.reshape(1).astype(jnp.int32), step_rate.reshape(1), params, large, halves, factors, small
    )


def solution(mesh):
    in_specs = (
        P("trial", "batch", None, None),
        P("trial", "batch", None, None),
        P(None, "batch", None),
        P(),
        P("trial"),
        P("trial", None, None),
        P("trial", None, None, None),
        P("trial", None, None, None),
        P("trial", None, None),
        P("trial", None, None),
        P("trial", None, None),
        P("trial", None),
        P("trial", None, None),
        P("trial", None),
    )
    out_specs = (
        P("trial", None, None),
        P("trial", None, None, None),
        P("trial", None, None, None),
        P("trial", None, None),
        P("trial", None, None),
        P("trial", None, None),
        P("trial", None),
        P("trial", None, None),
        P("trial", None),
    )
    return jax.shard_map(
        on_device, mesh=mesh, in_specs=in_specs, out_specs=out_specs, check_vma=False
    )
```

```python
import functools
import math

import jax
import jax.numpy as jnp
from jax import lax
from jax.experimental import pallas as pl
from jax.experimental.pallas import tpu as pltpu
from jax.sharding import PartitionSpec as P

W16 = 32
HID = 256
PAD = 24
DILATIONS = (6, 12, 18)
LANES = 128
RELATIVE = (0, -1, 1, 2)
BF16 = jnp.bfloat16
F32 = jnp.float32


def dot_nt(a, b):
    return lax.dot_general(a, b, (((1,), (1,)), ((), ())), preferred_element_type=F32)


def dot_nn(a, b):
    return lax.dot_general(a, b, (((1,), (0,)), ((), ())), preferred_element_type=F32)


def dot_exact(a, b):
    return lax.dot_general(
        a,
        b,
        (((1,), (0,)), ((), ())),
        precision=lax.Precision.HIGHEST,
        preferred_element_type=F32,
    )


def dot_exact_nt(a, b):
    return lax.dot_general(
        a,
        b,
        (((1,), (1,)), ((), ())),
        precision=lax.Precision.HIGHEST,
        preferred_element_type=F32,
    )


def dot_tn(a, b):
    return lax.dot_general(a, b, (((0,), (0,)), ((), ())), preferred_element_type=F32)


def taps_of_row(row, rows, dilation):
    taps = []
    for a in (-1, 0, 1):
        source = row + a * dilation
        if 0 <= source < rows:
            for b in (-1, 0, 1):
                taps.append((3 * (a + 1) + (b + 1), source, b * dilation))
    return taps


def clear_margins(padded):
    rows = padded.shape[0]
    blank = jnp.zeros((rows, PAD, LANES), F32)
    padded[:, 0:PAD, :] = blank
    padded[:, PAD + W16 : 2 * PAD + W16, :] = blank


def fill_padded(padded, x_ref, lanes):
    for row in range(padded.shape[0]):
        padded[row, PAD : PAD + W16, :] = x_ref[row * W16 : (row + 1) * W16, lanes].astype(F32)


def front_kernel(
    order,
    where_ref,
    piece0,
    piece1,
    piece2,
    piece3,
    marks,
    w_plain,
    w_depth,
    w_point,
    bias,
    w_proj,
    proj_bias,
    w_class,
    class_bias,
    maps_ref,
    joined_ref,
    dpre_ref,
    dz_ref,
    sums_ref,
    dclass_ref,
    padded,
):
    x_ref = maps_ref.at[0]
    x, y, z = where_ref[0], where_ref[1], where_ref[2]
    for outer, piece in enumerate((piece0, piece1, piece2, piece3)):
        for inner in range(4):
            far, near = RELATIVE[outer] + 4, RELATIVE[inner] + 4
            if order == 0:
                xx, yy = lax.rem(x + far, 4), lax.rem(y + near, 4)
            else:
                xx, yy = lax.rem(x + near, 4), lax.rem(y + far, 4)
            for k in range(2):
                zz = z if k == 0 else 1 - z
                start = pl.multiple_of((zz * 16 + yy * 4 + xx) * 16, 16)
                x_ref[pl.ds(start, 16), :] = piece[pl.ds((2 * inner + k) * 16, 16), :]
    rows = padded.shape[0]
    clear_margins(padded)

    def chunk(j, carry):
        lanes = pl.ds(pl.multiple_of(j * LANES, LANES), LANES)
        fill_padded(padded, x_ref, lanes)
        for k, dilation in enumerate(DILATIONS):
            for row in range(rows):
                total = jnp.zeros((W16, LANES), F32)
                for tap, source, shift in taps_of_row(row, rows, dilation):
                    weight = w_depth[9 * k + tap, :, lanes]
                    total = total + weight * padded[source, PAD + shift : PAD + shift + W16, :]
                maps_ref[k + 1, row * W16 : (row + 1) * W16, lanes] = total.astype(BF16)
        return carry

    lax.fori_loop(0, x_ref.shape[1] // LANES, chunk, 0)

    for branch in range(4):
        columns = slice(branch * HID, (branch + 1) * HID)
        if branch == 0:
            pre = dot_nt(x_ref[...], w_plain[...])
        else:
            pre = dot_nt(maps_ref[branch], w_point[branch - 1])
        joined_ref[:, columns] = jnp.maximum(pre + bias[:, columns], 0.0).astype(BF16)
    hidden = jnp.maximum(dot_nt(joined_ref[...], w_proj[...]) + proj_bias[...], 0.0).astype(BF16)
    logits = dot_nt(w_class[...], hidden) + class_bias[...]
    top = jnp.max(logits, axis=0, keepdims=True)
    raised = jnp.exp(logits - top)
    share = raised / jnp.sum(raised, axis=0, keepdims=True)
    class_ids = lax.broadcasted_iota(jnp.int32, logits.shape, 0)
    dlogits = share - jnp.where(class_ids == marks[...], 1.0, 0.0)
    square = (logits.shape[0], LANES)
    column = jnp.broadcast_to(jnp.sum(dlogits, axis=1, keepdims=True), square)
    on_diagonal = lax.broadcasted_iota(jnp.int32, square, 0) == lax.broadcasted_iota(
        jnp.int32, square, 1
    )
    short = dlogits.astype(BF16)
    dclass_ref[...] = dot_nn(short, hidden)
    dhidden = dot_tn(short, w_class[...])
    dpre = jnp.where(hidden.astype(F32) > 0, dhidden, 0.0)
    dpre_short = dpre.astype(BF16)
    dpre_ref[...] = dpre_short
    sums_ref[...] = jnp.zeros(sums_ref.shape, F32)
    sums_ref[3:4, 0:LANES] = jnp.sum(jnp.where(on_diagonal, column, 0.0), axis=0, keepdims=True)
    sums_ref[1:2, 0:HID] = jnp.sum(dpre_short.astype(F32), axis=0, keepdims=True)
    for branch in range(4):
        columns = slice(branch * HID, (branch + 1) * HID)
        djoined = dot_nn(dpre_short, w_proj[:, columns])
        dz = jnp.where(joined_ref[:, columns].astype(F32) > 0, djoined, 0.0).astype(BF16)
        dz_ref[:, columns] = dz
        sums_ref[0:1, columns] = jnp.sum(dz.astype(F32), axis=0, keepdims=True)


VMEM = pl.BlockSpec(memory_space=pltpu.VMEM)
SMEM = pl.BlockSpec(memory_space=pltpu.SMEM)


def front(order, where, pieces, marks, weights):
    pixels, channels = marks.shape[1], weights[0].shape[1]
    shapes = (
        ((4, pixels, channels), BF16),
        ((pixels, 4 * HID), BF16),
        ((pixels, HID), BF16),
        ((pixels, 4 * HID), BF16),
        ((8, 4 * HID), F32),
        ((32, HID), F32),
    )
    return pl.pallas_call(
        functools.partial(front_kernel, order),
        name="front",
        out_shape=[pltpu.VMEM(*shape) for shape in shapes],
        in_specs=[SMEM] + [VMEM] * (4 + 1 + len(weights)),
        out_specs=[VMEM] * len(shapes),
        scratch_shapes=[pltpu.VMEM((pixels // W16, 2 * PAD + W16, LANES), F32)],
        compiler_params=pltpu.CompilerParams(vmem_limit_bytes=16 * 2**20),
        cost_estimate=pl.CostEstimate(
            flops=6_700_000_000, bytes_accessed=12_000_000, transcendentals=16384
        ),
    )(where, *pieces, marks, *weights)


def taps_kernel(maps_ref, dz_ref, w_point, out_ref, padded, ddepth):
    x_ref = maps_ref.at[0]
    rows = padded.shape[1]
    halves = padded.shape[0]
    for half in range(halves):
        start = pl.multiple_of((pl.program_id(0) * halves + half) * LANES, LANES)
        clear_margins(padded.at[half])
        fill_padded(padded.at[half], x_ref, pl.ds(start, LANES))
    out_ref[...] = jnp.zeros(out_ref.shape, F32)
    for k, dilation in enumerate(DILATIONS):
        back = dot_nn(dz_ref[:, (k + 1) * HID : (k + 2) * HID], w_point[k])
        ddepth[k] = back.astype(BF16).astype(F32)
    for half in range(halves):
        lanes = slice(half * LANES, (half + 1) * LANES)
        for k, dilation in enumerate(DILATIONS):
            totals = {}
            for row in range(rows):
                slope = ddepth[k, row * W16 : (row + 1) * W16, lanes]
                for tap, source, shift in taps_of_row(row, rows, dilation):
                    value = slope * padded[half, source, PAD + shift : PAD + shift + W16, :]
                    value = jnp.sum(value.reshape(W16 // 8, 8, LANES), axis=0)
                    totals[tap] = value if tap not in totals else totals[tap] + value
            for tap, value in totals.items():
                out_ref[9 * k + tap : 9 * k + tap + 1, lanes] = jnp.sum(
                    value, axis=0, keepdims=True
                )


def depth_taps(maps, dz, w_point):
    pixels, channels = maps.shape[1:]
    block = 256
    return pl.pallas_call(
        taps_kernel,
        name="taps",
        grid=(channels // block,),
        out_shape=jax.ShapeDtypeStruct((32, channels), F32),
        in_specs=[
            VMEM,
            VMEM,
            pl.BlockSpec((3, HID, block), lambda j: (0, 0, j)),
        ],
        out_specs=pl.BlockSpec((32, block), lambda j: (0, j)),
        scratch_shapes=[
            pltpu.VMEM((block // LANES, pixels // W16, 2 * PAD + W16, LANES), F32),
            pltpu.VMEM((3, pixels, block), F32),
        ],
        compiler_params=pltpu.CompilerParams(vmem_limit_bytes=16 * 2**20),
        cost_estimate=pl.CostEstimate(
            flops=4_500_000_000, bytes_accessed=4_000_000, transcendentals=0
        ),
    )(maps, dz, w_point)


PRODUCT_COLUMNS = 512


def product_kernel(count, first, *refs):
    out_ref = refs[-1]
    layer, step = first + pl.program_id(0), pl.program_id(1)
    left_columns = pl.ds(pl.multiple_of(layer * HID, HID), HID)
    columns = pl.ds(pl.multiple_of(step * PRODUCT_COLUMNS, PRODUCT_COLUMNS), PRODUCT_COLUMNS)
    total = None
    for left, right in zip(refs[:count], refs[count : 2 * count]):
        right = right[layer, :, columns] if len(right.shape) == 3 else right[:, columns]
        part = dot_tn(left[:, left_columns], right)
        total = part if total is None else total + part
    out_ref[0] = total.astype(BF16)


def products(lefts, rights, first, layers):
    channels = rights[0].shape[-1]
    count = len(lefts)
    return pl.pallas_call(
        functools.partial(product_kernel, count, first),
        name="products",
        grid=(layers, channels // PRODUCT_COLUMNS),
        out_shape=jax.ShapeDtypeStruct((layers, HID, channels), BF16),
        in_specs=[VMEM] * (2 * count),
        out_specs=pl.BlockSpec((1, HID, PRODUCT_COLUMNS), lambda k, j: (k, 0, j)),
        compiler_params=pltpu.CompilerParams(vmem_limit_bytes=10 * 2**20),
        cost_estimate=pl.CostEstimate(
            flops=layers * 2_200_000_000, bytes_accessed=layers * 5_000_000, transcendentals=0
        ),
    )(*lefts, *rights)


STEPS = 8


def update_kernel(
    core_ref,
    rate_ref,
    w_plain,
    w_point,
    w_pool,
    w_proj,
    w_depth,
    b_branch,
    b_proj,
    w_class,
    b_class,
    mine0,
    rest0,
    mine1,
    rest1,
    mine2,
    rest2,
    factors,
    small,
    new_plain,
    new_point,
    new_pool,
    new_proj,
    new_depth,
    new_b_branch,
    new_b_proj,
    new_class,
    new_b_class,
    scale_ref,
    slopes_ref,
    left_ref,
):
    step = pl.program_id(0)
    pairs = ((mine0, rest0), (mine1, rest1), (mine2, rest2))
    count = factors.shape[0]
    arrays = (w_plain, w_point, w_pool, w_proj, w_depth, b_branch, b_proj, w_class, b_class)
    entries = sum(math.prod(array.shape) for array in arrays)

    def outer_squared(a, b):
        product = dot_exact_nt(a, a) * dot_exact_nt(b, b)
        return jnp.sum(product, keepdims=True)

    @pl.when(step == 0)
    def _():
        slopes_ref[...] = jnp.zeros(slopes_ref.shape, F32)
        slopes_ref[:count, :] = factors[:, : 2 * HID]
        left_ref[...] = slopes_ref[...].T
        total = jnp.zeros((16, small.shape[1]), F32)
        for mine, rest in pairs:
            for row in range(0, mine.shape[1], 16):
                for layer in range(mine.shape[0]):
                    one = mine[layer, row : row + 16, :].astype(F32)
                    other = rest[layer, row : row + 16, :].astype(F32)
                    total = total + (one * one + other * other)
        for row in range(0, small.shape[0], 16):
            total = total + jnp.square(small[row : row + 16, :])
        squares = jnp.sum(total, keepdims=True)
        squares = squares + outer_squared(factors[:, :HID], factors[:, 3 * HID :])
        squares = squares + outer_squared(
            factors[:, HID : 2 * HID], factors[:, 2 * HID : 3 * HID]
        )
        norm_scale = jnp.sqrt(squares / entries + 1e-06)
        scale_ref[...] = jnp.broadcast_to(rate_ref[0] / norm_scale, scale_ref.shape)

    scale = scale_ref[0:1, 0:1]

    def large(side):
        rows = new_plain.shape[1]
        here = pl.ds(pl.multiple_of(lax.rem(step, STEPS // 2) * rows, rows), rows)
        there = lax.rem(step + core_ref[0] * (STEPS // 2), STEPS)
        start = pl.multiple_of(there * rows, rows)
        there = pl.ds(start, rows)
        proj, low, high = (
            [pair[side][layer, here, :] for layer in range(pair[side].shape[0])] for pair in pairs
        )
        wide = proj[0].shape[-1]
        new_plain[0] = w_plain[0, there, :] - scale * low[0].astype(F32)
        new_point[0, 0] = w_point[0, 0, there, :] - scale * low[1].astype(F32)
        new_point[0, 1] = w_point[0, 1, there, :] - scale * high[0].astype(F32)
        new_point[0, 2] = w_point[0, 2, there, :] - scale * high[1].astype(F32)
        new_proj[0, :, :wide] = w_proj[0, there, :wide] - scale * proj[0].astype(F32)
        proj4_grad = dot_exact(left_ref[pl.ds(HID + start, rows), :count], factors[:, 2 * HID : 3 * HID])
        new_proj[0, :, wide:] = w_proj[0, there, wide:] - scale * proj4_grad
        pool_grad = dot_exact(left_ref[pl.ds(start, rows), :count], factors[:, 3 * HID :])
        new_pool[0] = w_pool[0, there, :] - scale * pool_grad

    @pl.when(step < STEPS // 2)
    def _():
        large(0)

    @pl.when(step >= STEPS // 2)
    def _():
        large(1)

    @pl.when(step == 0)
    def _():
        for row in range(w_depth.shape[0]):
            new_depth[row] = w_depth[row] - scale * small[row : row + 1, :]
        for branch in range(5):
            row = 32 if branch < 4 else 34
            first = branch % 4 * HID
            new_b_branch[branch] = (
                b_branch[branch] - scale * small[row : row + 1, first : first + HID]
            )
        new_b_proj[...] = b_proj[...] - scale * small[33:34, :HID]
        classes = w_class.shape[0]
        for index in range(classes):
            row, first = 40 + index % 8, index // 8 * HID
            new_class[index] = w_class[index] - scale * small[row : row + 1, first : first + HID]
        new_b_class[...] = b_class[...] - scale * small[35:36, :classes]


def fetch_kernel(*refs):
    count = len(refs) // 3
    copies = [
        pltpu.make_async_copy(source, target, done)
        for source, target, done in zip(refs[:count], refs[count : 2 * count], refs[2 * count :])
    ]
    for copy in copies:
        copy.start()
    for copy in copies:
        copy.wait()


def fetch(arrays):
    return pl.pallas_call(
        fetch_kernel,
        name="fetch",
        out_shape=[pltpu.VMEM(array.shape, array.dtype) for array in arrays],
        in_specs=[pl.BlockSpec(memory_space=pl.ANY)] * len(arrays),
        out_specs=[VMEM] * len(arrays),
        scratch_shapes=[pltpu.SemaphoreType.DMA] * len(arrays),
        compiler_params=pltpu.CompilerParams(vmem_limit_bytes=2**20),
        cost_estimate=pl.CostEstimate(
            flops=3_500_000_000, bytes_accessed=8_000_000, transcendentals=0
        ),
    )(*arrays)


def update(core, rate, params, large, halves, factors, small):
    w_plain, w_depth, w_point, w_pool, b_branch, w_proj, b_proj, w_class, b_class = params
    inputs = tuple(large) + tuple(
        array if array.ndim == 2 else array.reshape(-1, 1, array.shape[-1])
        for array in (w_depth, b_branch, b_proj, w_class, b_class)
    )
    rows, half = HID // STEPS, STEPS // 2

    def where(step, core_ref):
        return lax.rem(step + core_ref[0] * half, STEPS)

    def by_rows(shape):
        if len(shape) == 2:
            return pl.BlockSpec((rows, shape[1]), lambda j, core: (where(j, core), 0))
        if len(shape) == 3:
            return pl.BlockSpec((1, rows, shape[2]), lambda j, core: (0, where(j, core), 0))
        return pl.BlockSpec((1, shape[1], rows, shape[3]), lambda j, core: (0, 0, where(j, core), 0))

    def whole(shape):
        return pl.BlockSpec(shape, lambda j, core: (0,) * len(shape))

    small_specs = [whole(array.shape) for array in inputs[4:]]
    specs = [by_rows(array.shape) for array in inputs[:4]] + small_specs
    new = pl.pallas_call(
        update_kernel,
        name="update",
        out_shape=[jax.ShapeDtypeStruct(array.shape, F32) for array in inputs],
        grid_spec=pltpu.PrefetchScalarGridSpec(
            num_scalar_prefetch=1,
            grid=(STEPS,),
            in_specs=[SMEM]
            + [VMEM] * 4
            + small_specs
            + [VMEM] * (2 * len(halves))
            + [VMEM, VMEM],
            out_specs=specs,
            scratch_shapes=[
                pltpu.VMEM((8, LANES), F32),
                pltpu.VMEM((LANES, 2 * HID), F32),
                pltpu.VMEM((2 * HID, LANES), F32),
            ],
        ),
        compiler_params=pltpu.CompilerParams(vmem_limit_bytes=14 * 2**20),
        cost_estimate=pl.CostEstimate(
            flops=4_000_000, bytes_accessed=20_000_000, transcendentals=0
        ),
    )(core, rate, *inputs, *(array for pair in halves for array in pair), factors, small)
    order = (0, 4, 1, 2, 5, 3, 6, 7, 8)
    return tuple(new[i].reshape(param.shape) for i, param in zip(order, params))


def place(z, y, x):
    return z * 16 + (y % 4) * 4 + x % 4


EVERY = [(z, y, x) for z in range(2) for y in range(4) for x in range(4)]


def along_x(step):
    return [(place(z, y, x), place(z, y, x + step)) for z, y, x in EVERY]


def along_y(step):
    return [(place(z, y, x), place(z, y + step, x)) for z, y, x in EVERY]


ACROSS_Z = [(t, (t + 16) % 32) for t in range(32)]
CORES = [(b, b ^ 1) for b in range(4)]
CHIPS = [(b, b ^ 2) for b in range(4)]


def gather_ring(block, along):
    return (
        block,
        lax.ppermute(block, "trial", along(1)),
        lax.ppermute(block, "trial", along(-1)),
        lax.ppermute(block, "trial", along(2)),
    )


def from_batch(mine):
    return [mine] + [
        lax.ppermute(mine, "batch", [(b, b ^ other) for b in range(4)]) for other in (1, 2, 3)
    ]


def in_order(parts, core, chip):
    near, beside, across, beyond = parts
    low = jnp.where(core == 0, jnp.concatenate([near, beside]), jnp.concatenate([beside, near]))
    high = jnp.where(core == 0, jnp.concatenate([across, beyond]), jnp.concatenate([beyond, across]))
    return jnp.where(chip == 0, jnp.concatenate([low, high]), jnp.concatenate([high, low]))


def sum_cores(partial, core):
    half = partial.shape[1] // 2
    mine = lax.dynamic_slice_in_dim(partial, core * half, half, 1)
    other = lax.dynamic_slice_in_dim(partial, (1 - core) * half, half, 1)
    return (mine.astype(F32) + lax.ppermute(other, "batch", CORES).astype(F32)).astype(BF16)


def sum_chips(pair):
    return (pair.astype(F32) + lax.ppermute(pair, "batch", CHIPS).astype(F32)).astype(BF16)


def sum_batch_small(partial):
    pair = partial.astype(F32) + lax.ppermute(partial, "batch", CORES).astype(F32)
    pair = pair.astype(BF16)
    return pair.astype(F32) + lax.ppermute(pair, "batch", CHIPS).astype(F32)


def pick(table, plan, turn_ids):
    return jnp.stack(
        [lax.dynamic_index_in_dim(table, plan[m], 0, keepdims=False) for m in turn_ids]
    )


def pool_map(coarse):
    return (jnp.sum(coarse, axis=-1, dtype=F32) / coarse.shape[-1]).astype(BF16)


def on_device(
    features16,
    features32,
    labels,
    plan,
    lr_index,
    w_plain,
    w_depth,
    w_point,
    w_pool,
    b_branch,
    w_proj,
    b_proj,
    w_class,
    b_class,
):
    turns = plan.shape[0]
    trial = lax.axis_index("trial")
    batch = lax.axis_index("batch")
    core, chip = batch % 2, batch // 2
    where = jnp.stack([trial % 4, (trial // 4) % 4, trial // 16]).astype(jnp.int32)

    own = features16[0, 0].T
    channels = own.shape[1]
    pieces = lax.all_to_all(own.reshape(32, 16, channels), "trial", 0, 0, tiled=True)
    turn_lists = [list(range(order, turns, 2)) for order in range(2)]
    picked = pick(pieces, plan, turn_lists[0] + turn_lists[1])
    pooled = pool_map(features32[0, 0]).reshape(-1, 1, channels)
    pooled = jnp.where((plan == trial)[None, :, None], pooled, jnp.zeros((), BF16))
    pooled = pooled.reshape(-1, channels)
    rows = pooled.shape[0]
    across = lax.ppermute(
        jnp.concatenate([picked.reshape(-1, channels), pooled]), "trial", ACROSS_Z
    )
    pooled = pooled + across[-rows:]
    across = across[:-rows].reshape(picked.shape)
    blocks, outers = [None] * turns, [None] * turns
    for order, (inner, outer) in enumerate(((along_y, along_x), (along_x, along_y))):
        turn_ids = turn_lists[order]
        count = len(turn_ids)
        some = slice(order * len(turn_lists[0]), order * len(turn_lists[0]) + count)
        block = jnp.stack([picked[some], across[some]], axis=1).reshape(-1, channels)
        size = block.shape[0]
        if order == 0:
            block = jnp.concatenate([block, pooled])
        ring = gather_ring(block, inner)
        if order == 0:
            pooled = sum(part[size:] for part in ring)
        for place_in, m in enumerate(turn_ids):
            first, last = place_in * size // count, (place_in + 1) * size // count
            parts = [part[first:last] for part in ring]
            blocks[m] = jnp.concatenate(parts + [pooled] if m == 0 else parts)
            outers[m] = outer
    after = lax.optimization_barrier
    maps = [gather_ring(blocks[m], outers[m]) for m in range(2)]
    pooled = sum(part[4 * size // count :] for part in maps[0])
    pooled = [pooled[first : first + turns] for first in range(0, rows, turns)]

    point16 = w_point[0].astype(BF16)
    proj16 = w_proj[0].astype(BF16)
    taps = w_depth.reshape(27, 1, -1)
    classes = w_class.shape[1]
    class16 = jnp.pad(w_class[0].astype(BF16), ((0, 32 - classes), (0, 0)))
    class_bias = jnp.pad(b_class[0], (0, 32 - classes), constant_values=-1e30)[:, None]
    wide = 4 * HID
    pool16 = w_pool[0].astype(BF16)
    branch4 = sum(
        dot_nt(part, pool16[:, i * channels : (i + 1) * channels]) for i, part in enumerate(pooled)
    )
    branch4 = jax.nn.relu(branch4 + b_branch[0, 4]).astype(BF16)
    proj_bias = dot_nt(branch4, proj16[:, wide:]) + b_proj[0]
    marks = pick(labels[:, 0], plan, range(turns))

    fronts = []
    for m in range(turns):
        if m >= 2:
            maps.append(gather_ring(blocks[m], outers[m]))
        weights = (
            w_plain[0].astype(BF16),
            taps,
            point16,
            b_branch[0, :4].reshape(1, wide),
            proj16[:, :wide],
            proj_bias[m : m + 1],
            class16,
            class_bias,
        )
        if m == 0:
            maps[0], blocks[2] = after((maps[0], blocks[2]))
        fronts.append(front(m % 2, where, maps[m], marks[m : m + 1], weights))
        if m == 0:
            fronts[0], maps[1], blocks[3] = after((fronts[0], maps[1], blocks[3]))
    stacks, joined, dpres, dzs, sums, dclass = zip(*fronts)

    dbias_proj = jnp.stack([part[1, :HID] for part in sums])
    dbranch4 = dot_exact(dbias_proj, proj16[:, wide:].astype(F32))
    dbranch4 = jnp.where(branch4 > 0, dbranch4, 0.0)
    factors = [dbranch4, dbias_proj, branch4] + pooled
    factors = jnp.concatenate([part.astype(F32) for part in factors], axis=1)
    factors = from_batch(factors)
    proj_part = products(dpres, joined, 0, 1)
    proj_pair = sum_cores(proj_part, core)
    dzs, proj_pair = after((dzs, proj_pair))
    low_part = products(dzs, stacks, 0, 2)
    proj_total = sum_chips(proj_pair)
    dzs, low_part, proj_total = after((dzs, low_part, proj_total))
    low_pair = sum_cores(low_part, core)
    high_part = products(dzs, stacks, 2, 2)
    dzs, high_part, low_pair, factors = after((dzs, high_part, low_pair, factors))
    high_pair = sum_cores(high_part, core)
    low_total = sum_chips(low_pair)
    taps_parts = [depth_taps(stacks[0], dzs[0], point16)]
    dzs, taps_parts, high_pair = after((dzs, taps_parts, high_pair))
    taps_parts.append(depth_taps(stacks[1], dzs[1], point16))
    dzs, taps_parts, proj_total = after((dzs, taps_parts, proj_total))
    proj_rest = lax.ppermute(proj_total, "batch", CORES)
    taps_parts.append(depth_taps(stacks[2], dzs[2], point16))
    dzs, taps_parts, proj_rest = after((dzs, taps_parts, proj_rest))
    taps_parts.append(depth_taps(stacks[3], dzs[3], point16))
    depth_part = sum(taps_parts)
    factors, depth_part = after((factors, depth_part))
    factors = [jnp.pad(part, ((0, 8 - turns), (0, 0))) for part in factors]
    factors = in_order(factors, core, chip)
    dclass = sum(dclass)
    bias_row = jnp.pad(jnp.sum(dbranch4, axis=0)[None], ((2, 5), (0, wide - HID)))
    small = jnp.concatenate(
        [
            depth_part,
            sum(sums) + bias_row,
            jnp.concatenate([dclass[8 * g : 8 * g + 8] for g in range(4)], axis=1),
        ]
    )
    small = sum_batch_small(small.astype(BF16))
    high_other = lax.ppermute(high_pair, "batch", CHIPS)
    large, factors = after(((w_plain, w_point, w_pool, w_proj), factors))
    high_other, low_total, large, small = after((high_other, low_total, fetch(large), small))
    high_total = (high_pair.astype(F32) + high_other.astype(F32)).astype(BF16)
    halves = [(proj_total, proj_rest)]
    halves += [(total, lax.ppermute(total, "batch", CORES)) for total in (low_total, high_total)]

    params = (w_plain, w_depth, w_point, w_pool, b_branch, w_proj, b_proj, w_class, b_class)

    step_rate = 0.5 * jnp.exp2(-6.0 * lr_index[0].astype(F32) / 1073741824.0)
    return update(
        core.reshape(1).astype(jnp.int32), step_rate.reshape(1), params, large, halves, factors, small
    )


def solution(mesh):
    in_specs = (
        P("trial", "batch", None, None),
        P("trial", "batch", None, None),
        P(None, "batch", None),
        P(),
        P("trial"),
        P("trial", None, None),
        P("trial", None, None, None),
        P("trial", None, None, None),
        P("trial", None, None),
        P("trial", None, None),
        P("trial", None, None),
        P("trial", None),
        P("trial", None, None),
        P("trial", None),
    )
    out_specs = (
        P("trial", None, None),
        P("trial", None, None, None),
        P("trial", None, None, None),
        P("trial", None, None),
        P("trial", None, None),
        P("trial", None, None),
        P("trial", None),
        P("trial", None, None),
        P("trial", None),
    )
    return jax.shard_map(
        on_device, mesh=mesh, in_specs=in_specs, out_specs=out_specs, check_vma=False
    )
```
